32 devices in a mesh: wide: 8 (over y, x, core), narrow: 4 (over z).
Axes of the slice: x: 2, y: 2, z: 4, core: 2. Of those that a mesh axis runs over, the one named last changes fastest.
Arguments:
- inputs: bfloat16 [32768, 2048], P('wide', 'narrow'), may hold values from -6 to 6
- flags: int32 [32768], replicated, may hold values from 0 to 1, as said below
- w_one: bfloat16 [2048, 2048], P(None, 'narrow'), may hold values from -0.125 to 0.125
- gamma_one: float32 [2048], P(('narrow', 'wide')), may hold values from 0.1 to 0.4
- beta_one: float32 [2048], P(('narrow', 'wide')), may hold values from -0.2 to 0.2
- decay_one: float32 [2048], P(('narrow', 'wide')), may hold values from 0.9 to 1
- w_two: bfloat16 [2048, 2048], P(None, 'narrow'), may hold values from -0.125 to 0.125
- gamma_two: float32 [2048], P(('narrow', 'wide')), may hold values from 0.1 to 0.4
- beta_two: float32 [2048], P(('narrow', 'wide')), may hold values from -0.2 to 0.2
- decay_two: float32 [2048], P(('narrow', 'wide')), may hold values from 0.9 to 1
- cotangent: bfloat16 [32768, 2048], P('wide', 'narrow'), may hold values from -6 to 6
Outputs:
- output: bfloat16 [32768, 2048], P('wide', 'narrow')
- grad_inputs: float32 [32768, 2048], P('wide', 'narrow')
- grad_w_one: float32 [2048, 2048], P('wide', 'narrow')
- grad_gamma_one: float32 [2048], P(('narrow', 'wide'))
- grad_beta_one: float32 [2048], P(('narrow', 'wide'))
- grad_decay_one: float32 [2048], P(('narrow', 'wide'))
- grad_w_two: float32 [2048, 2048], P('wide', 'narrow')
- grad_gamma_two: float32 [2048], P(('narrow', 'wide'))
- grad_beta_two: float32 [2048], P(('narrow', 'wide'))
- grad_decay_two: float32 [2048], P(('narrow', 'wide'))
The draws below stay inside these ranges and needn't reach their ends.
Inputs may be any that keep to these rules, and one draw needn't show every extreme that they name: flags is 1 at the first frame of each clip and 0 elsewhere; each row of 512 frames begins a clip, and no clip crosses a row's end; every clip holds 64 to 512 frames, except a row's last, which may be shorter.
All inputs are finite; a program needn't handle non-finite values.
Results may differ from the reference program's by a relative error of at most 0.0068.
Values may be sent and summed in bfloat16 or wider, within the bound.
No kernel may reach another device: no remote copies, remote signals or barrier semaphores. Data moves between devices by JAX's collectives and lax.ppermute only.
A program may use at most 448 MiB of HBM per device.

```python
import math
import jax
import jax.numpy as jnp
from jax import lax

H = 2048
ROW_LEN = 512
SEG_MIN = 64
ROWS = 64
FRAMES = 32768


def draw_flags(key, part):
    key = jax.random.fold_in(key, 11)
    per_row = ROW_LEN // SEG_MIN + 1
    lengths = jax.random.randint(key, (ROWS, per_row), SEG_MIN, ROW_LEN + 1)
    lengths = lengths.at[0, 0].set(ROW_LEN)
    lengths = lengths.at[1, 0].set(SEG_MIN)
    starts = jnp.cumsum(lengths, axis=1) - lengths
    starts = jnp.where(starts < ROW_LEN, starts, ROW_LEN)
    places = jnp.arange(ROW_LEN, dtype=jnp.int32)
    marked = jnp.any(starts[:, :, None] == places[None, None, :], axis=1)
    return marked.astype(jnp.int32).reshape(ROWS * ROW_LEN)


def level_of(own_key, shape, pieces, smallest, high):
    factor_of = 1.0
    for position, shards_of in pieces:
        heights = jax.random.uniform(jax.random.fold_in(jax.random.fold_in(own_key, 6), position), (shards_of,), jnp.float32, smallest / len(pieces), high / len(pieces))
        factor_of = factor_of * jnp.repeat(jnp.exp(heights), shape[position] // shards_of).reshape((-1,) + (1,) * (len(shape) - 1 - position))
    return factor_of


def normal_values(own_key, extent, deviation, bound, shards=(), held_as=jnp.bfloat16):
    values = jax.random.normal(own_key, extent, jnp.float32) * deviation
    if len(shards) > 0:
        values = level_of(own_key, extent, shards, -0.22, 0.18) * values
    return jnp.clip(values, min=-bound, max=bound).astype(held_as)


def setup_inputs(seed: int = 0) -> dict:
    splits = jax.random.split(jax.random.key(seed), 12)
    return {
        "inputs": normal_values(splits[0], (FRAMES, H), 1.0, 6.0, ((0, 8), (1, 4))),
        "flags": draw_flags(jax.random.fold_in(splits[11], 71), 0),
        "w_one": normal_values(splits[2], (H, H), H ** -0.5, 0.125, ((1, 4),)),
        "gamma_one": jnp.clip(jnp.exp(math.log(0.4) - 1.3862944 * jax.random.uniform(splits[3], (H,), jnp.float32) ** level_of(splits[3], (H,), ((0, 32),), -0.2, 0.2)), 0.1, 0.4),
        "beta_one": normal_values(splits[4], (H,), 0.05, 0.2, ((0, 32),), jnp.float32),
        "decay_one": jnp.clip(0.9 + 0.100000024 * jax.random.uniform(splits[5], (H,), jnp.float32) ** level_of(splits[5], (H,), ((0, 32),), -0.2, 0.2), 0.9, 1.0),
        "w_two": normal_values(splits[6], (H, H), H ** -0.5, 0.125, ((1, 4),)),
        "gamma_two": jnp.clip(jnp.exp(math.log(0.4) - 1.3862944 * jax.random.uniform(splits[7], (H,), jnp.float32) ** level_of(splits[7], (H,), ((0, 32),), -0.2, 0.2)), 0.1, 0.4),
        "beta_two": normal_values(splits[8], (H,), 0.05, 0.2, ((0, 32),), jnp.float32),
        "decay_two": jnp.clip(0.9 + 0.100000024 * jax.random.uniform(splits[9], (H,), jnp.float32) ** level_of(splits[9], (H,), ((0, 32),), -0.2, 0.2), 0.9, 1.0),
        "cotangent": normal_values(splits[10], (FRAMES, H), 1.0, 6.0, ((0, 8), (1, 4))),
    }


@jax.custom_vjp
def low(v):
    return lax.optimization_barrier(v.astype(jnp.bfloat16)).astype(jnp.float32)

@jax.custom_vjp
def low_back(v):
    return v

def low_keep(v):
    return (low(v), None)

def low_pass(kept, grad):
    return (grad,)

def back_keep(v):
    return (v, None)

def back_low(kept, grad):
    return (low(grad),)
low.defvjp(low_keep, low_pass)
low_back.defvjp(back_keep, back_low)
epsilon = 1e-05

def run_rows(normed_values, decay, keep):
    chans = normed_values.shape[1]
    seq = jnp.transpose(normed_values.reshape(ROWS, ROW_LEN, chans), (1, 0, 2))
    hold = jnp.transpose(keep.reshape(ROWS, ROW_LEN))
    span = math.gcd(ROW_LEN, 64)
    blocks = ROW_LEN // span
    seq = seq.reshape(blocks, span, ROWS, chans)
    hold = hold.reshape(blocks, span, ROWS)

    def step(state, item):
        value, mark = item
        fresh = jax.nn.softplus(value + decay * state * mark[:, None])
        return (fresh, fresh)

    def block(state, items):
        return lax.scan(step, state, items)
    start = jnp.zeros((ROWS, chans), jnp.float32)
    _, hidden_states = lax.scan(jax.checkpoint(block), start, (seq, hold))
    hidden_states = hidden_states.reshape(ROW_LEN, ROWS, chans)
    return jnp.transpose(hidden_states, (1, 0, 2)).reshape(FRAMES, chans)

def layer(source, weight, gamma, beta, decay, keep):
    proj = jnp.dot(source, weight, precision=lax.Precision.HIGHEST)
    proj = low_back(low(proj))
    mean = lax.optimization_barrier(jnp.mean(proj, 0))
    centered_values = proj - mean
    var = lax.optimization_barrier(jnp.mean(centered_values * centered_values, 0))
    normed_values = gamma * (centered_values * lax.rsqrt(var + epsilon)) + beta
    hidden_states = run_rows(normed_values, decay, keep)
    return low_back(low(hidden_states))

def reference(inputs, flags, w_one, gamma_one, beta_one, decay_one, w_two, gamma_two, beta_two, decay_two, cotangent):
    keep = (1 - flags).astype(jnp.float32)

    def forward(source, wa, ga, ba, da, wb, gb, bb, db):
        first = layer(source, wa, ga, ba, da, keep)
        second = layer(first, wb, gb, bb, db, keep)
        return source + second
    primal = (inputs.astype(jnp.float32), w_one.astype(jnp.float32), gamma_one, beta_one, decay_one, w_two.astype(jnp.float32), gamma_two, beta_two, decay_two)
    result, pull = jax.vjp(forward, *primal)
    grads = pull(cotangent.astype(jnp.float32))
    return (result.astype(jnp.bfloat16), grads[0], grads[1], grads[2], grads[3], grads[4], grads[5], grads[6], grads[7], grads[8])
```

```python
import functools

import jax
import jax.numpy as jnp
from jax import lax
from jax.experimental import pallas as pl
from jax.experimental.pallas import tpu as pltpu
from jax.sharding import PartitionSpec as P

ROW_LEN = 512
EPSILON = 1e-05
LOG2E = 1.4426950408889634
LN2 = 0.6931471805599453
LANES = 128
SUB = 16
CHUNK = 64
VMEM_LIMIT = 56 * 2**20
BOTH = ("narrow", "wide")

params_of = functools.partial(pltpu.CompilerParams, vmem_limit_bytes=VMEM_LIMIT)
SMEM = pl.BlockSpec(memory_space=pltpu.SMEM)
BRIEF = pl.CostEstimate(flops=1, bytes_accessed=1, transcendentals=0)


def whole(shape):
    return pl.BlockSpec(shape, lambda *_: (0,) * len(shape))


def swap(blocks):
    return lax.all_to_all(blocks, "narrow", split_axis=0, concat_axis=0)


def merge_all(value, merge, axis, size):
    k = 1
    while k < size:
        other = lax.ppermute(value, axis, [(i, i ^ k) for i in range(size)])
        value = merge(value, other)
        k *= 2
    return value


def add(a, b):
    return a + b


def merge_moments(frames):
    count = [frames]

    def merge(a, b):
        gap = a[0:1] - b[0:1]
        squares = a[1:2] + b[1:2] + gap * gap * (count[0] / 2)
        count[0] *= 2
        means = (a + b) * 0.5
        return jnp.concatenate([means[0:1], squares, means[2:3], a[3:] + b[3:]])

    return merge


def gather_rows(weights, wide):
    rows = weights[0].shape[0] // wide
    first = lax.axis_index("wide") * rows
    shares = [lax.dynamic_slice_in_dim(weight, first, rows, 0) for weight in weights]
    both = lax.all_gather(jnp.concatenate(shares, 0), "narrow", axis=1, tiled=True)
    return [both[i * rows : (i + 1) * rows] for i in range(len(weights))]


def project_kernel(groups, x_refs, w_ref, z_ref, moments_ref, joined_ref=None):
    frames, cols = z_ref.shape
    here = pl.program_id(0)
    step = min(256, frames)
    sums = jnp.zeros((1, cols), jnp.float32)
    for m in range(0, frames, step):
        acc = None
        for ref, lo, count, feature in groups:
            if not lo <= m < lo + count:
                continue
            x_ref = x_refs[ref]
            block, first, depth = feature
            x = x_ref[block, m - lo : m - lo + step, :]
            term = jnp.dot(x, w_ref[first : first + depth, :], preferred_element_type=jnp.float32)
            acc = term if acc is None else acc + term
        rounded = acc.astype(jnp.bfloat16)
        z_ref[m : m + step, :] = rounded
        sums += jnp.sum(rounded.astype(jnp.float32), 0, keepdims=True)
    mean = sums / frames
    squares = jnp.zeros((1, cols), jnp.float32)
    for m in range(0, frames, step):
        gap = z_ref[m : m + step, :].astype(jnp.float32) - mean
        squares += jnp.sum(gap * gap, 0, keepdims=True)
    at = pl.ds(pl.multiple_of(here * cols, cols), cols)
    moments_ref[0:1, at] = mean
    moments_ref[1:2, at] = squares
    if joined_ref is None:
        own = x_refs[0][0, :, at].astype(jnp.float32)
        moments_ref[2:3, at] = jnp.sum(own, 0, keepdims=True) / frames
        return
    total = jnp.zeros((1, joined_ref.shape[1]), jnp.float32)
    lo = 0
    for x_ref in x_refs:
        count = x_ref.shape[1]
        own = x_ref[here]
        joined_ref[lo : lo + count, :] = own
        total += jnp.sum(own.astype(jnp.float32), 0, keepdims=True)
        lo += count
    place = pl.ds(pl.multiple_of(here * joined_ref.shape[1], joined_ref.shape[1]), joined_ref.shape[1])
    moments_ref[2:3, place] = total / frames


def project(pieces, weight):
    blocks, _, depth = pieces[0].shape
    frames = sum(p.shape[1] for p in pieces)
    rows, cols = weight.shape
    joined = blocks > 1
    steps = blocks if joined else 4
    width = cols // steps
    groups = []
    lo = 0
    for i, p in enumerate(pieces):
        groups += [(i, lo, p.shape[1], (k, k * depth, depth)) for k in range(blocks)]
        lo += p.shape[1]
    out_shape = [
        jax.ShapeDtypeStruct((frames, cols), jnp.bfloat16),
        jax.ShapeDtypeStruct((3, cols), jnp.float32),
    ]
    out_specs = [pl.BlockSpec((frames, width), lambda i: (0, i)), whole((3, cols))]
    if joined:
        out_shape.append(jax.ShapeDtypeStruct((frames, rows), jnp.bfloat16))
        out_specs.append(pl.BlockSpec((frames, depth), lambda i: (0, i)))

    def kernel(*refs):
        project_kernel(groups, refs[: len(pieces)], *refs[len(pieces) :])

    return pl.pallas_call(
        kernel,
        grid=(steps,),
        in_specs=[whole(p.shape) for p in pieces]
        + [pl.BlockSpec((rows, width), lambda i: (0, i))],
        out_specs=out_specs,
        out_shape=out_shape,
        compiler_params=params_of(),
        cost_estimate=BRIEF,
        name="project",
    )(*pieces, weight)


def to_steps(row_ref, lanes_ref, tiles):
    for j in range(tiles):
        lanes_ref[j : j + 1, :] = row_ref[:, j * LANES : (j + 1) * LANES]


def forward_kernel(total_frames, ranges, keep, moments, gains, z_ref, s_ref, *refs):
    parts = len(ranges)
    h_refs, (vec, state, seq) = refs[:parts], refs[parts:]
    rows, chunk, width = z_ref.shape
    tiles = width // LANES

    @pl.when(pl.program_id(0) == 0)
    def _():
        scale = gains[0:1, :] * lax.rsqrt(moments[1:2, :] / total_frames + EPSILON)
        lanes = [moments[0:1, :], scale * LOG2E, gains[1:2, :] * LOG2E, gains[2:3, :] * LOG2E]
        for i, row in enumerate(lanes):
            for j in range(tiles):
                vec[i, j : j + 1, :] = row[:, j * LANES : (j + 1) * LANES]
        state[...] = jnp.zeros_like(state)

    mean, scale, shift, decay = (vec[i] for i in range(4))
    first = pl.program_id(0) * chunk

    def block(c, running):
        running = list(running)
        for r in range(rows):
            values = z_ref[r, pl.ds(pl.multiple_of(c * SUB, SUB), SUB), :].astype(jnp.float32)
            for j in range(tiles):
                for half in range(SUB // 8):
                    seq[r, pl.ds(half * 8 * tiles + j, 8, stride=tiles), :] = values[
                        half * 8 : half * 8 + 8, j * LANES : (j + 1) * LANES
                    ]
        for k in range(SUB):
            for r in range(rows):
                value = (seq[r, k * tiles : (k + 1) * tiles, :] - mean) * scale + shift
                before = value + (decay * keep[r, first + c * SUB + k]) * running[r]
                fresh = jnp.where(
                    before > 30.0, before * LN2, jnp.log(1.0 + jnp.exp2(before))
                )
                running[r] = fresh
                s_ref[r, pl.ds(pl.multiple_of((c * SUB + k) * tiles, tiles), tiles), :] = fresh
        for r in range(rows):
            for (lo, hi), h_ref in zip(ranges, h_refs, strict=True):
                per_block = tiles // h_ref.shape[0]
                for q in range(h_ref.shape[0]):
                    for j in range(lo, hi):
                        tile = q * per_block + j
                        halves = [
                            s_ref[
                                r,
                                pl.ds((c * SUB + half * 8) * tiles + tile, 8, stride=tiles),
                                :,
                            ]
                            for half in range(SUB // 8)
                        ]
                        h_ref[
                            q,
                            r,
                            pl.ds(pl.multiple_of(c * SUB, SUB), SUB),
                            (j - lo) * LANES : (j - lo + 1) * LANES,
                        ] = jnp.concatenate(halves, 0).astype(jnp.bfloat16)
        return tuple(running)

    running = lax.fori_loop(0, chunk // SUB, block, tuple(state[r] for r in range(rows)))
    for r in range(rows):
        state[r] = running[r]


def forward(z, moments, gains, keep, blocks, ranges, total_frames):
    rows, length = keep.shape
    width = z.shape[1]
    tiles = width // LANES
    results = pl.pallas_call(
        functools.partial(forward_kernel, total_frames, ranges),
        grid=(length // CHUNK,),
        in_specs=[
            SMEM,
            whole((3, width)),
            whole((3, width)),
            pl.BlockSpec((rows, CHUNK, width), lambda i: (0, i, 0)),
        ],
        out_specs=[pl.BlockSpec((rows, CHUNK * tiles, LANES), lambda i: (0, i, 0))]
        + [
            pl.BlockSpec((blocks, rows, CHUNK, (hi - lo) * LANES), lambda i: (0, 0, i, 0))
            for lo, hi in ranges
        ],
        out_shape=[jax.ShapeDtypeStruct((rows, length * tiles, LANES), jnp.float32)]
        + [
            jax.ShapeDtypeStruct((blocks, rows, length, (hi - lo) * LANES), jnp.bfloat16)
            for lo, hi in ranges
        ],
        scratch_shapes=[
            pltpu.VMEM((4, tiles, LANES), jnp.float32),
            pltpu.VMEM((rows, tiles, LANES), jnp.float32),
            pltpu.VMEM((rows, SUB * tiles, LANES), jnp.float32),
        ],
        compiler_params=params_of(),
        cost_estimate=BRIEF,
        name="forward",
    )(keep, moments, gains, z.reshape(rows, length, width))
    return results[0], [h.reshape(blocks, rows * length, -1) for h in results[1:]]


def backward_kernel(ranges, keep, moments, gains, s_ref, before_ref, z_ref, *refs):
    parts = len(ranges)
    g_refs, (dpre_ref, sums_ref, vec, state, seq, grads) = refs[:parts], refs[parts:]
    rows, chunk, width = z_ref.shape
    tiles = width // LANES
    step = pl.program_id(0)
    first = (pl.num_programs(0) - 1 - step) * chunk

    @pl.when(step == 0)
    def _():
        for j in range(tiles):
            vec[j : j + 1, :] = gains[2:3, j * LANES : (j + 1) * LANES]
        state[...] = jnp.zeros_like(state)
        sums_ref[...] = jnp.zeros_like(sums_ref)

    decay = vec[...]
    mean = moments[0:1, :]
    blocks = chunk // SUB

    def block(i, running):
        *running, dsum = running
        c = blocks - 1 - i
        base = pl.multiple_of(c * SUB, SUB)
        for r in range(rows):
            for (lo, hi), g_ref in zip(ranges, g_refs, strict=True):
                per_block = tiles // g_ref.shape[0]
                for q in range(g_ref.shape[0]):
                    values = g_ref[q, r, pl.ds(base, SUB), :].astype(jnp.float32)
                    for j in range(lo, hi):
                        tile = q * per_block + j
                        for half in range(SUB // 8):
                            seq[r, pl.ds(half * 8 * tiles + tile, 8, stride=tiles), :] = values[
                                half * 8 : half * 8 + 8, (j - lo) * LANES : (j - lo + 1) * LANES
                            ]
        for k in range(SUB - 1, -1, -1):
            for r in range(rows):
                at = c * SUB + k
                s = s_ref[r, pl.ds(pl.multiple_of(at * tiles, tiles), tiles), :]
                if k > 0:
                    prior = s_ref[r, pl.ds(pl.multiple_of((at - 1) * tiles, tiles), tiles), :]
                else:
                    inner = s_ref[
                        r, pl.ds(pl.multiple_of(jnp.maximum(at - 1, 0) * tiles, tiles), tiles), :
                    ]
                    prior = jnp.where(c > 0, inner, before_ref[r])
                mark = keep[r, first + at]
                slope = 1.0 - jnp.exp2(s * -LOG2E)
                dpre = (seq[r, k * tiles : (k + 1) * tiles, :] + running[r]) * slope
                held = dpre * mark
                running[r] = held * decay
                dsum = dsum + held * prior
                grads[r, k * tiles : (k + 1) * tiles, :] = dpre
        gb = jnp.zeros((8, width), jnp.float32)
        gg = jnp.zeros((8, width), jnp.float32)
        for r in range(rows):
            gaps = z_ref[r, pl.ds(base, SUB), :].astype(jnp.float32) - mean
            for half in range(SUB // 8):
                dpre = jnp.concatenate(
                    [
                        grads[r, pl.ds(half * 8 * tiles + j, 8, stride=tiles), :]
                        for j in range(tiles)
                    ],
                    1,
                )
                dpre_ref[r, pl.ds(pl.multiple_of(base + half * 8, 8), 8), :] = dpre
                gb += dpre
                gg += dpre * gaps[half * 8 : half * 8 + 8, :]
        sums_ref[0:8, :] += gb
        sums_ref[8:16, :] += gg
        return (*running, dsum)

    start = tuple(state[r] for r in range(rows)) + (state[rows],)
    *running, dsum = lax.fori_loop(0, blocks, block, start)
    for r in range(rows):
        state[r] = running[r]
    state[rows] = dsum

    @pl.when(step == pl.num_programs(0) - 1)
    def _():
        gb = jnp.sum(sums_ref[0:8, :], 0, keepdims=True)
        gg = jnp.sum(sums_ref[8:16, :], 0, keepdims=True)
        sums_ref[0:1, :] = gb
        sums_ref[1:2, :] = gg
        for j in range(tiles):
            sums_ref[2:3, j * LANES : (j + 1) * LANES] = state[rows, j : j + 1, :]


def backward(grads, ranges, states, z, moments, gains, keep):
    rows, length = keep.shape
    width = z.shape[1]
    tiles = width // LANES
    blocks = grads[0].shape[0]
    last = length // CHUNK - 1
    dpre, sums = pl.pallas_call(
        functools.partial(backward_kernel, ranges),
        grid=(length // CHUNK,),
        in_specs=[
            SMEM,
            whole((3, width)),
            whole((3, width)),
            pl.BlockSpec((rows, CHUNK * tiles, LANES), lambda i: (0, last - i, 0)),
            pl.BlockSpec(
                (rows, tiles, LANES), lambda i: (0, jnp.maximum((last - i) * CHUNK - 1, 0), 0)
            ),
            pl.BlockSpec((rows, CHUNK, width), lambda i: (0, last - i, 0)),
        ]
        + [
            pl.BlockSpec((blocks, rows, CHUNK, (hi - lo) * LANES), lambda i: (0, 0, last - i, 0))
            for lo, hi in ranges
        ],
        out_specs=[
            pl.BlockSpec((rows, CHUNK, width), lambda i: (0, last - i, 0)),
            whole((16, width)),
        ],
        out_shape=[
            jax.ShapeDtypeStruct((rows, length, width), jnp.float32),
            jax.ShapeDtypeStruct((16, width), jnp.float32),
        ],
        scratch_shapes=[
            pltpu.VMEM((tiles, LANES), jnp.float32),
            pltpu.VMEM((rows + 1, tiles, LANES), jnp.float32),
            pltpu.VMEM((rows, SUB * tiles, LANES), jnp.float32),
            pltpu.VMEM((rows, SUB * tiles, LANES), jnp.float32),
        ],
        compiler_params=params_of(),
        cost_estimate=BRIEF,
        name="backward",
    )(
        keep,
        moments,
        gains,
        states,
        states,
        z.reshape(rows, length, width),
        *[g.reshape(blocks, rows, length, -1) for g in grads],
    )
    return dpre.reshape(rows * length, width), sums[0:3]


def dproject_kernel(total_frames, moments, gains, sums, dpre_ref, z_ref, w_ref, dz_ref, level_ref, da_ref):
    rstd = lax.rsqrt(moments[1:2, :] / total_frames + EPSILON)
    scale = gains[0:1, :] * rstd
    level = sums[0:1, :] / total_frames
    slope = sums[1:2, :] * (rstd * rstd) / total_frames
    gap = z_ref[...].astype(jnp.float32) - moments[0:1, :]
    dz = (scale * (dpre_ref[...] - level - gap * slope)).astype(jnp.bfloat16)
    dz_ref[...] = dz
    here = jnp.sum(dz.astype(jnp.float32), 0, keepdims=True)

    @pl.when(pl.program_id(0) == 0)
    def _():
        level_ref[...] = here

    @pl.when(pl.program_id(0) > 0)
    def _():
        level_ref[...] += here

    parts = da_ref.shape[0]
    depth = w_ref.shape[0] // parts
    for p in range(parts):
        da_ref[p] = lax.dot_general(
            dz_ref[...],
            w_ref[p * depth : (p + 1) * depth, :],
            (((1,), (1,)), ((), ())),
            preferred_element_type=jnp.float32,
        ).astype(jnp.bfloat16)


def dproject(dpre, z, moments, gains, sums, weight, parts, total_frames):
    frames, width = z.shape
    rows = weight.shape[0]
    step = min(256, frames)
    return pl.pallas_call(
        functools.partial(dproject_kernel, total_frames),
        grid=(frames // step,),
        in_specs=[
            whole((3, width)),
            whole((3, width)),
            whole((3, width)),
            pl.BlockSpec((step, width), lambda i: (i, 0)),
            pl.BlockSpec((step, width), lambda i: (i, 0)),
            whole((rows, width)),
        ],
        out_specs=[
            pl.BlockSpec((step, width), lambda i: (i, 0)),
            whole((1, width)),
            pl.BlockSpec((parts, step, rows // parts), lambda i: (0, i, 0)),
        ],
        out_shape=[
            jax.ShapeDtypeStruct((frames, width), jnp.bfloat16),
            jax.ShapeDtypeStruct((1, width), jnp.float32),
            jax.ShapeDtypeStruct((parts, frames, rows // parts), jnp.bfloat16),
        ],
        compiler_params=params_of(),
        cost_estimate=BRIEF,
        name="dproject",
    )(moments, gains, sums, dpre, z, weight)


def weight_kernel(level, source_ref, dz_ref, center_ref, out_ref):
    terms = lax.dot_general(
        source_ref[...], dz_ref[...], (((0,), (0,)), ((), ())), preferred_element_type=jnp.float32
    )
    out_ref[...] = (terms - center_ref[...] * level[...]).astype(jnp.bfloat16)


def weight_terms(source, center, dz, level):
    frames, rows = source.shape
    cols = dz.shape[1]
    tile = 256
    return pl.pallas_call(
        weight_kernel,
        grid=(rows // tile,),
        in_specs=[
            whole((1, cols)),
            pl.BlockSpec((frames, tile), lambda i: (0, i)),
            whole((frames, cols)),
            pl.BlockSpec((tile, 1), lambda i: (i, 0)),
        ],
        out_specs=pl.BlockSpec((tile, cols), lambda i: (i, 0)),
        out_shape=jax.ShapeDtypeStruct((rows, cols), jnp.bfloat16),
        compiler_params=params_of(),
        cost_estimate=BRIEF,
        name="weight",
    )(level, source, dz, center.reshape(rows, 1))


def per_device(sizes, inputs, flags, w_one, *rest):
    gamma_one, beta_one, decay_one, w_two, gamma_two, beta_two, decay_two, cotangent = rest
    wide, narrow = sizes["wide"], sizes["narrow"]
    n = lax.axis_index("narrow")
    w = lax.axis_index("wide")
    frames = inputs.shape[0] // narrow
    part = inputs.shape[1]
    tiles = part // LANES
    total_frames = inputs.shape[0] * wide
    rows = frames // ROW_LEN
    first = w * inputs.shape[0] + n * frames
    keep = lax.dynamic_slice_in_dim(flags, first, frames, 0).reshape(rows, ROW_LEN)
    keep = (1 - keep).astype(jnp.float32)
    tie = lax.optimization_barrier

    def along(value, merge):
        return merge_all(value, merge, "narrow", narrow)

    def across(value, merge):
        return merge_all(value, merge, "wide", wide)

    own = jnp.stack([gamma_one, beta_one, decay_one, gamma_two, beta_two, decay_two])
    each = own.shape[1]
    spread = jnp.zeros((6, each * wide * narrow), jnp.float32)
    spread = lax.dynamic_update_slice_in_dim(spread, own, (n * wide + w) * each, 1)

    groups = [(0, tiles // 4), (tiles // 4, 3 * tiles // 4), (3 * tiles // 4, tiles)]

    def columns(held, g):
        lo, hi = groups[g]
        return swap(held[:, lo * LANES : hi * LANES].reshape(narrow, frames, -1))

    split = frames // 4
    held = inputs.reshape(narrow, frames, part)
    piece = swap(held[:, :split])
    share_one, share_two = gather_rows([w_one, w_two], wide)
    share_one, share_two, held = tie((share_one, share_two, held))
    pieces = [piece, swap(held[:, split:])]
    full_one = lax.all_gather(share_one, "wide", axis=0, tiled=True)
    full_one, share_two = tie((full_one, share_two))
    full_two = lax.all_gather(share_two, "wide", axis=0, tiled=True)

    pieces, held = tie((pieces, cotangent))
    group = columns(held, 0)
    z_one, moments, source = project(pieces, full_one)
    moments, group = tie((moments, group))
    grads = [group]
    moments = jnp.concatenate([moments, spread])
    merge = merge_moments(frames)
    moments = along(moments, merge)
    moments, held = tie((moments, cotangent))
    group = columns(held, 1)
    moments_one = across(moments, merge)
    gains_one, gains_two = moments_one[3:6], moments_one[6:9]
    moments_one = moments_one[:3]
    every = [(0, z_one.shape[1] // LANES)]
    states_one, (h_one,) = forward(
        z_one, moments_one, gains_one, keep, 1, every, total_frames
    )
    z_two, moments = project([h_one], full_two)
    moments, group = tie((moments, group))
    grads.append(group)
    merge = merge_moments(frames)
    moments = along(moments, merge)
    moments, held = tie((moments, cotangent))
    group = columns(held, 2)
    moments_two = across(moments, merge)
    states_two, h_two = forward(
        z_two, moments_two, gains_two, keep, narrow, groups, total_frames
    )
    h_two, group = tie((h_two, group))
    grads.append(group)

    second = [swap(h_two[0])]
    dpre, sums = backward(grads, groups, states_two, z_two, moments_two, gains_two, keep)
    sums, second[0] = tie((sums, second[0]))
    sums = along(sums, add)
    sums, h_two = tie((sums, h_two))
    group = swap(h_two[1])
    sums_two = across(sums, add)
    dz_two, level_two, dh_one = dproject(
        dpre, z_two, moments_two, gains_two, sums_two, full_two, 1, total_frames
    )
    dpre, sums = backward([dh_one], every, states_one, z_one, moments_one, gains_one, keep)
    own_level_two = level_two
    sums = jnp.concatenate([sums, level_two], 0)
    sums, group = tie((sums, group))
    second.append(group)
    sums = along(sums, add)
    sums, h_two = tie((sums, h_two))
    group = swap(h_two[2])
    sums_one = across(sums, add)
    level_two = sums_one[3:]
    sums_one = sums_one[:3]
    dz_one, level_one, dsource = dproject(
        dpre, z_one, moments_one, gains_one, sums_one, full_one, narrow, total_frames
    )
    dsource, group, dz_one, dz_two = tie((dsource, group, dz_one, dz_two))
    second.append(group)
    arrived = swap(dsource).reshape(inputs.shape)

    whole_two = jnp.concatenate(second, axis=2).reshape(inputs.shape).astype(jnp.float32)
    output = (inputs.astype(jnp.float32) + whole_two).astype(jnp.bfloat16)

    center_one, center_two = moments_one[2], moments_two[2]
    terms_two = weight_terms(h_one[0], center_two, dz_two, own_level_two)
    terms_one = weight_terms(source, center_one, dz_one, level_one)
    level_one = along(across(level_one, add), add)
    grad_inputs = cotangent.astype(jnp.float32) + arrived.astype(jnp.float32)

    def summed(terms, center, level):
        plane = lax.psum_scatter(terms, "wide", scatter_dimension=0, tiled=True)
        span = plane.shape[0]
        blocks = plane.reshape(span, narrow, part).transpose(1, 0, 2)
        weight = jnp.sum(swap(blocks).astype(jnp.float32), 0)
        rows_of = lax.dynamic_slice_in_dim(center, w * span, span, 0)
        cols_of = lax.dynamic_slice_in_dim(level[0], n * part, part, 0)
        return weight + rows_of[:, None] * cols_of[None, :]

    dw_two = summed(terms_two, center_two, level_two)
    dw_one = summed(terms_one, center_one, level_one)

    def small(sums, moments):
        rstd = lax.rsqrt(moments[1] / total_frames + EPSILON)
        whole_ones = (sums[1] * rstd, sums[0], sums[2])
        return [lax.dynamic_slice_in_dim(v, (n * wide + w) * each, each, 0) for v in whole_ones]

    return (
        output,
        grad_inputs,
        dw_one,
        *small(sums_one, moments_one),
        dw_two,
        *small(sums_two, moments_two),
    )


def solution(mesh):
    neurons = P(("narrow", "wide"))
    frames = P("wide", "narrow")
    weight = P(None, "narrow")
    small = (neurons, neurons, neurons)
    return jax.shard_map(
        functools.partial(per_device, dict(mesh.shape)),
        mesh=mesh,
        in_specs=(frames, P(), weight, *small, weight, *small, frames),
        out_specs=(frames, frames, frames, *small, frames, *small),
        check_vma=False,
    )
```

```python
import functools

import jax
import jax.numpy as jnp
from jax import lax
from jax.experimental import pallas as pl
from jax.experimental.pallas import tpu as pltpu
from jax.sharding import PartitionSpec as P

ROW_LEN = 512
EPSILON = 1e-05
LOG2E = 1.4426950408889634
LN2 = 0.6931471805599453
LANES = 128
SUB = 16
CHUNK = 64
VMEM_LIMIT = 56 * 2**20
BOTH = ("narrow", "wide")

params_of = functools.partial(pltpu.CompilerParams, vmem_limit_bytes=VMEM_LIMIT)
SMEM = pl.BlockSpec(memory_space=pltpu.SMEM)
BRIEF = pl.CostEstimate(flops=1, bytes_accessed=1, transcendentals=0)


def whole(shape):
    return pl.BlockSpec(shape, lambda *_: (0,) * len(shape))


def swap(blocks):
    return lax.all_to_all(blocks, "narrow", split_axis=0, concat_axis=0)


def merge_all(value, merge, axis, size):
    k = 1
    while k < size:
        other = lax.ppermute(value, axis, [(i, i ^ k) for i in range(size)])
        value = merge(value, other)
        k *= 2
    return value


def add(a, b):
    return a + b


def merge_moments(frames):
    count = [frames]

    def merge(a, b):
        row = lax.broadcasted_iota(jnp.int32, a.shape, 0)
        scale = jnp.where((row == 0) | (row == 2), 0.5, 1.0)
        gap = a[0:1] - b[0:1]
        squares = gap * gap * (count[0] / 2)
        count[0] *= 2
        return (a + b) * scale + jnp.where(row == 1, squares, 0.0)

    return merge


def gather_rows(weights, wide):
    rows = weights[0].shape[0] // wide
    first = lax.axis_index("wide") * rows
    shares = [lax.dynamic_slice_in_dim(weight, first, rows, 0) for weight in weights]
    both = lax.all_gather(jnp.concatenate(shares, 0), "narrow", axis=1, tiled=True)
    return [both[i * rows : (i + 1) * rows] for i in range(len(weights))]


def project_kernel(groups, x_refs, w_ref, z_ref, moments_ref, joined_ref=None):
    frames, cols = z_ref.shape
    here = pl.program_id(0)
    step = min(256, frames)
    sums = jnp.zeros((1, cols), jnp.float32)
    for m in range(0, frames, step):
        acc = None
        for ref, lo, count, feature in groups:
            if not lo <= m < lo + count:
                continue
            x_ref = x_refs[ref]
            block, first, depth = feature
            x = x_ref[block, m - lo : m - lo + step, :]
            term = jnp.dot(x, w_ref[first : first + depth, :], preferred_element_type=jnp.float32)
            acc = term if acc is None else acc + term
        rounded = acc.astype(jnp.bfloat16)
        z_ref[m : m + step, :] = rounded
        sums += jnp.sum(rounded.astype(jnp.float32), 0, keepdims=True)
    mean = sums / frames
    squares = jnp.zeros((1, cols), jnp.float32)
    for m in range(0, frames, step):
        gap = z_ref[m : m + step, :].astype(jnp.float32) - mean
        squares += jnp.sum(gap * gap, 0, keepdims=True)
    at = pl.ds(pl.multiple_of(here * cols, cols), cols)
    moments_ref[0:1, at] = mean
    moments_ref[1:2, at] = squares
    if joined_ref is None:
        own = x_refs[0][0, :, at].astype(jnp.float32)
        moments_ref[2:3, at] = jnp.sum(own, 0, keepdims=True) / frames
        return
    total = jnp.zeros((1, joined_ref.shape[1]), jnp.float32)
    lo = 0
    for x_ref in x_refs:
        count = x_ref.shape[1]
        own = x_ref[here]
        joined_ref[lo : lo + count, :] = own
        total += jnp.sum(own.astype(jnp.float32), 0, keepdims=True)
        lo += count
    place = pl.ds(pl.multiple_of(here * joined_ref.shape[1], joined_ref.shape[1]), joined_ref.shape[1])
    moments_ref[2:3, place] = total / frames


def project(pieces, weight):
    blocks, _, depth = pieces[0].shape
    frames = sum(p.shape[1] for p in pieces)
    rows, cols = weight.shape
    joined = blocks > 1
    steps = blocks if joined else 4
    width = cols // steps
    groups = []
    lo = 0
    for i, p in enumerate(pieces):
        groups += [(i, lo, p.shape[1], (k, k * depth, depth)) for k in range(blocks)]
        lo += p.shape[1]
    out_shape = [
        jax.ShapeDtypeStruct((frames, cols), jnp.bfloat16),
        jax.ShapeDtypeStruct((3, cols), jnp.float32),
    ]
    out_specs = [pl.BlockSpec((frames, width), lambda i: (0, i)), whole((3, cols))]
    if joined:
        out_shape.append(jax.ShapeDtypeStruct((frames, rows), jnp.bfloat16))
        out_specs.append(pl.BlockSpec((frames, depth), lambda i: (0, i)))

    def kernel(*refs):
        project_kernel(groups, refs[: len(pieces)], *refs[len(pieces) :])

    return pl.pallas_call(
        kernel,
        grid=(steps,),
        in_specs=[whole(p.shape) for p in pieces]
        + [pl.BlockSpec((rows, width), lambda i: (0, i))],
        out_specs=out_specs,
        out_shape=out_shape,
        compiler_params=params_of(),
        cost_estimate=BRIEF,
        name="project",
    )(*pieces, weight)


def to_steps(row_ref, lanes_ref, tiles):
    for j in range(tiles):
        lanes_ref[j : j + 1, :] = row_ref[:, j * LANES : (j + 1) * LANES]


def forward_kernel(total_frames, ranges, keep, moments, gains, z_ref, s_ref, *refs):
    parts = len(ranges)
    h_refs, (vec, state, seq) = refs[:parts], refs[parts:]
    rows, chunk, width = z_ref.shape
    tiles = width // LANES

    @pl.when(pl.program_id(0) == 0)
    def _():
        scale = gains[0:1, :] * lax.rsqrt(moments[1:2, :] / total_frames + EPSILON)
        lanes = [moments[0:1, :], scale * LOG2E, gains[1:2, :] * LOG2E, gains[2:3, :] * LOG2E]
        for i, row in enumerate(lanes):
            for j in range(tiles):
                vec[i, j : j + 1, :] = row[:, j * LANES : (j + 1) * LANES]
        state[...] = jnp.zeros_like(state)

    mean, scale, shift, decay = (vec[i] for i in range(4))
    first = pl.program_id(0) * chunk

    def block(c, running):
        running = list(running)
        for r in range(rows):
            values = z_ref[r, pl.ds(pl.multiple_of(c * SUB, SUB), SUB), :].astype(jnp.float32)
            for j in range(tiles):
                for half in range(SUB // 8):
                    seq[r, pl.ds(half * 8 * tiles + j, 8, stride=tiles), :] = values[
                        half * 8 : half * 8 + 8, j * LANES : (j + 1) * LANES
                    ]
        for k in range(SUB):
            for r in range(rows):
                value = (seq[r, k * tiles : (k + 1) * tiles, :] - mean) * scale + shift
                before = value + (decay * keep[r, first + c * SUB + k]) * running[r]
                fresh = jnp.where(
                    before > 30.0, before * LN2, jnp.log(1.0 + jnp.exp2(before))
                )
                running[r] = fresh
                s_ref[r, pl.ds(pl.multiple_of((c * SUB + k) * tiles, tiles), tiles), :] = fresh
        for r in range(rows):
            for (lo, hi), h_ref in zip(ranges, h_refs, strict=True):
                per_block = tiles // h_ref.shape[0]
                for q in range(h_ref.shape[0]):
                    for j in range(lo, hi):
                        tile = q * per_block + j
                        halves = [
                            s_ref[
                                r,
                                pl.ds((c * SUB + half * 8) * tiles + tile, 8, stride=tiles),
                                :,
                            ]
                            for half in range(SUB // 8)
                        ]
                        h_ref[
                            q,
                            r,
                            pl.ds(pl.multiple_of(c * SUB, SUB), SUB),
                            (j - lo) * LANES : (j - lo + 1) * LANES,
                        ] = jnp.concatenate(halves, 0).astype(jnp.bfloat16)
        return tuple(running)

    running = lax.fori_loop(0, chunk // SUB, block, tuple(state[r] for r in range(rows)))
    for r in range(rows):
        state[r] = running[r]


def forward(z, moments, gains, keep, blocks, ranges, total_frames):
    rows, length = keep.shape
    width = z.shape[1]
    tiles = width // LANES
    results = pl.pallas_call(
        functools.partial(forward_kernel, total_frames, ranges),
        grid=(length // CHUNK,),
        in_specs=[
            SMEM,
            whole((3, width)),
            whole((3, width)),
            pl.BlockSpec((rows, CHUNK, width), lambda i: (0, i, 0)),
        ],
        out_specs=[pl.BlockSpec((rows, CHUNK * tiles, LANES), lambda i: (0, i, 0))]
        + [
            pl.BlockSpec((blocks, rows, CHUNK, (hi - lo) * LANES), lambda i: (0, 0, i, 0))
            for lo, hi in ranges
        ],
        out_shape=[jax.ShapeDtypeStruct((rows, length * tiles, LANES), jnp.float32)]
        + [
            jax.ShapeDtypeStruct((blocks, rows, length, (hi - lo) * LANES), jnp.bfloat16)
            for lo, hi in ranges
        ],
        scratch_shapes=[
            pltpu.VMEM((4, tiles, LANES), jnp.float32),
            pltpu.VMEM((rows, tiles, LANES), jnp.float32),
            pltpu.VMEM((rows, SUB * tiles, LANES), jnp.float32),
        ],
        compiler_params=params_of(),
        cost_estimate=BRIEF,
        name="forward",
    )(keep, moments, gains, z.reshape(rows, length, width))
    return results[0], [h.reshape(blocks, rows * length, -1) for h in results[1:]]


def backward_kernel(ranges, keep, moments, gains, s_ref, before_ref, z_ref, *refs):
    parts = len(ranges)
    g_refs, (dpre_ref, sums_ref, vec, state, seq, grads) = refs[:parts], refs[parts:]
    rows, chunk, width = z_ref.shape
    tiles = width // LANES
    step = pl.program_id(0)
    first = (pl.num_programs(0) - 1 - step) * chunk

    @pl.when(step == 0)
    def _():
        for j in range(tiles):
            vec[j : j + 1, :] = gains[2:3, j * LANES : (j + 1) * LANES]
        state[...] = jnp.zeros_like(state)
        sums_ref[...] = jnp.zeros_like(sums_ref)

    decay = vec[...]
    mean = moments[0:1, :]
    blocks = chunk // SUB

    def block(i, running):
        *running, dsum = running
        c = blocks - 1 - i
        base = pl.multiple_of(c * SUB, SUB)
        for r in range(rows):
            for (lo, hi), g_ref in zip(ranges, g_refs, strict=True):
                per_block = tiles // g_ref.shape[0]
                for q in range(g_ref.shape[0]):
                    values = g_ref[q, r, pl.ds(base, SUB), :].astype(jnp.float32)
                    for j in range(lo, hi):
                        tile = q * per_block + j
                        for half in range(SUB // 8):
                            seq[r, pl.ds(half * 8 * tiles + tile, 8, stride=tiles), :] = values[
                                half * 8 : half * 8 + 8, (j - lo) * LANES : (j - lo + 1) * LANES
                            ]
        for k in range(SUB - 1, -1, -1):
            for r in range(rows):
                at = c * SUB + k
                s = s_ref[r, pl.ds(pl.multiple_of(at * tiles, tiles), tiles), :]
                if k > 0:
                    prior = s_ref[r, pl.ds(pl.multiple_of((at - 1) * tiles, tiles), tiles), :]
                else:
                    inner = s_ref[
                        r, pl.ds(pl.multiple_of(jnp.maximum(at - 1, 0) * tiles, tiles), tiles), :
                    ]
                    prior = jnp.where(c > 0, inner, before_ref[r])
                mark = keep[r, first + at]
                slope = 1.0 - jnp.exp2(s * -LOG2E)
                dpre = (seq[r, k * tiles : (k + 1) * tiles, :] + running[r]) * slope
                held = dpre * mark
                running[r] = held * decay
                dsum = dsum + held * prior
                grads[r, k * tiles : (k + 1) * tiles, :] = dpre
        gb = jnp.zeros((8, width), jnp.float32)
        gg = jnp.zeros((8, width), jnp.float32)
        for r in range(rows):
            gaps = z_ref[r, pl.ds(base, SUB), :].astype(jnp.float32) - mean
            for half in range(SUB // 8):
                dpre = jnp.concatenate(
                    [
                        grads[r, pl.ds(half * 8 * tiles + j, 8, stride=tiles), :]
                        for j in range(tiles)
                    ],
                    1,
                )
                dpre_ref[r, pl.ds(pl.multiple_of(base + half * 8, 8), 8), :] = dpre
                gb += dpre
                gg += dpre * gaps[half * 8 : half * 8 + 8, :]
        sums_ref[0:8, :] += gb
        sums_ref[8:16, :] += gg
        return (*running, dsum)

    start = tuple(state[r] for r in range(rows)) + (state[rows],)
    *running, dsum = lax.fori_loop(0, blocks, block, start)
    for r in range(rows):
        state[r] = running[r]
    state[rows] = dsum

    @pl.when(step == pl.num_programs(0) - 1)
    def _():
        gb = jnp.sum(sums_ref[0:8, :], 0, keepdims=True)
        gg = jnp.sum(sums_ref[8:16, :], 0, keepdims=True)
        sums_ref[0:1, :] = gb
        sums_ref[1:2, :] = gg
        for j in range(tiles):
            sums_ref[2:3, j * LANES : (j + 1) * LANES] = state[rows, j : j + 1, :]


def backward(grads, ranges, states, z, moments, gains, keep):
    rows, length = keep.shape
    width = z.shape[1]
    tiles = width // LANES
    blocks = grads[0].shape[0]
    last = length // CHUNK - 1
    dpre, sums = pl.pallas_call(
        functools.partial(backward_kernel, ranges),
        grid=(length // CHUNK,),
        in_specs=[
            SMEM,
            whole((3, width)),
            whole((3, width)),
            pl.BlockSpec((rows, CHUNK * tiles, LANES), lambda i: (0, last - i, 0)),
            pl.BlockSpec(
                (rows, tiles, LANES), lambda i: (0, jnp.maximum((last - i) * CHUNK - 1, 0), 0)
            ),
            pl.BlockSpec((rows, CHUNK, width), lambda i: (0, last - i, 0)),
        ]
        + [
            pl.BlockSpec((blocks, rows, CHUNK, (hi - lo) * LANES), lambda i: (0, 0, last - i, 0))
            for lo, hi in ranges
        ],
        out_specs=[
            pl.BlockSpec((rows, CHUNK, width), lambda i: (0, last - i, 0)),
            whole((16, width)),
        ],
        out_shape=[
            jax.ShapeDtypeStruct((rows, length, width), jnp.float32),
            jax.ShapeDtypeStruct((16, width), jnp.float32),
        ],
        scratch_shapes=[
            pltpu.VMEM((tiles, LANES), jnp.float32),
            pltpu.VMEM((rows + 1, tiles, LANES), jnp.float32),
            pltpu.VMEM((rows, SUB * tiles, LANES), jnp.float32),
            pltpu.VMEM((rows, SUB * tiles, LANES), jnp.float32),
        ],
        compiler_params=params_of(),
        cost_estimate=BRIEF,
        name="backward",
    )(
        keep,
        moments,
        gains,
        states,
        states,
        z.reshape(rows, length, width),
        *[g.reshape(blocks, rows, length, -1) for g in grads],
    )
    return dpre.reshape(rows * length, width), sums[0:3]


def dproject_kernel(total_frames, moments, gains, sums, dpre_ref, z_ref, w_ref, dz_ref, level_ref, da_ref):
    rstd = lax.rsqrt(moments[1:2, :] / total_frames + EPSILON)
    scale = gains[0:1, :] * rstd
    level = sums[0:1, :] / total_frames
    slope = sums[1:2, :] * (rstd * rstd) / total_frames
    gap = z_ref[...].astype(jnp.float32) - moments[0:1, :]
    dz = (scale * (dpre_ref[...] - level - gap * slope)).astype(jnp.bfloat16)
    dz_ref[...] = dz
    here = jnp.sum(dz.astype(jnp.float32), 0, keepdims=True)

    @pl.when(pl.program_id(0) == 0)
    def _():
        level_ref[...] = here

    @pl.when(pl.program_id(0) > 0)
    def _():
        level_ref[...] += here

    parts = da_ref.shape[0]
    depth = w_ref.shape[0] // parts
    for p in range(parts):
        da_ref[p] = lax.dot_general(
            dz_ref[...],
            w_ref[p * depth : (p + 1) * depth, :],
            (((1,), (1,)), ((), ())),
            preferred_element_type=jnp.float32,
        ).astype(jnp.bfloat16)


def dproject(dpre, z, moments, gains, sums, weight, parts, total_frames, lo, hi):
    width = z.shape[1]
    rows = weight.shape[0]
    step = min(256, hi - lo)
    frames = hi - lo
    return pl.pallas_call(
        functools.partial(dproject_kernel, total_frames),
        grid=(frames // step,),
        in_specs=[
            whole((3, width)),
            whole((3, width)),
            whole((3, width)),
            pl.BlockSpec((step, width), lambda i: (i + lo // step, 0)),
            pl.BlockSpec((step, width), lambda i: (i + lo // step, 0)),
            whole((rows, width)),
        ],
        out_specs=[
            pl.BlockSpec((step, width), lambda i: (i, 0)),
            whole((1, width)),
            pl.BlockSpec((parts, step, rows // parts), lambda i: (0, i, 0)),
        ],
        out_shape=[
            jax.ShapeDtypeStruct((frames, width), jnp.bfloat16),
            jax.ShapeDtypeStruct((1, width), jnp.float32),
            jax.ShapeDtypeStruct((parts, frames, rows // parts), jnp.bfloat16),
        ],
        compiler_params=params_of(),
        cost_estimate=BRIEF,
        name="dproject",
    )(moments, gains, sums, dpre, z, weight)


def weight_kernel(pieces, *refs):
    level_refs, dz_refs = refs[:pieces], refs[pieces : 2 * pieces]
    center_ref, source_ref, out_ref = refs[2 * pieces :]
    level = sum(level_ref[...] for level_ref in level_refs)
    center = jnp.transpose(jnp.broadcast_to(center_ref[...], (8, center_ref.shape[1])))[:, :1]
    terms = -center * level
    lo = 0
    for dz_ref in dz_refs:
        count = dz_ref.shape[0]
        terms += lax.dot_general(
            source_ref[lo : lo + count, :],
            dz_ref[...],
            (((0,), (0,)), ((), ())),
            preferred_element_type=jnp.float32,
        )
        lo += count
    out_ref[...] = terms.astype(jnp.bfloat16)


def weight_terms(source, center, dz, levels):
    frames, rows = source.shape
    cols = dz[0].shape[1]
    tile = 256
    return pl.pallas_call(
        functools.partial(weight_kernel, len(dz)),
        grid=(rows // tile,),
        in_specs=[whole((1, cols))] * len(dz)
        + [whole(d.shape) for d in dz]
        + [
            pl.BlockSpec((1, tile), lambda i: (0, i)),
            pl.BlockSpec((frames, tile), lambda i: (0, i)),
        ],
        out_specs=pl.BlockSpec((tile, cols), lambda i: (i, 0)),
        out_shape=jax.ShapeDtypeStruct((rows, cols), jnp.bfloat16),
        compiler_params=params_of(),
        cost_estimate=BRIEF,
        name="weight",
    )(*levels, *dz, center, source)


def per_device(sizes, inputs, flags, w_one, *rest):
    gamma_one, beta_one, decay_one, w_two, gamma_two, beta_two, decay_two, cotangent = rest
    wide, narrow = sizes["wide"], sizes["narrow"]
    n = lax.axis_index("narrow")
    w = lax.axis_index("wide")
    frames = inputs.shape[0] // narrow
    part = inputs.shape[1]
    tiles = part // LANES
    total_frames = inputs.shape[0] * wide
    rows = frames // ROW_LEN
    first = w * inputs.shape[0] + n * frames
    keep = lax.dynamic_slice_in_dim(flags, first, frames, 0).reshape(rows, ROW_LEN)
    keep = (1 - keep).astype(jnp.float32)
    tie = lax.optimization_barrier

    def along(value, merge):
        return merge_all(value, merge, "narrow", narrow)

    def across(value, merge):
        return merge_all(value, merge, "wide", wide)

    own = jnp.stack([gamma_one, beta_one, decay_one, gamma_two, beta_two, decay_two])
    each = own.shape[1]
    spread = jnp.zeros((6, each * wide * narrow), jnp.float32)
    spread = lax.dynamic_update_slice_in_dim(spread, own, (n * wide + w) * each, 1)

    groups_in = [(0, tiles // 4), (tiles // 4, 3 * tiles // 4), (3 * tiles // 4, tiles)]
    groups_out = groups_in

    held = [
        cotangent[:, lo * LANES : hi * LANES].reshape(narrow, frames, -1) for lo, hi in groups_in
    ]

    split = frames // 4
    blocks = inputs.reshape(narrow, frames, part)
    early, late = blocks[:, :split], blocks[:, split:]
    early = swap(early)
    share_one, share_two = gather_rows([w_one, w_two], wide)
    share_one, share_two, early, late, held = tie((share_one, share_two, early, late, held))
    late = swap(late)
    full_one = lax.all_gather(share_one, "wide", axis=0, tiled=True)
    late, held, share_two = tie((late, held, share_two))
    full_two = lax.all_gather(share_two, "wide", axis=0, tiled=True)
    group = swap(held[0])
    z_one, moments, source = project([early, late], full_one)
    moments, group = tie((moments, group))
    grads = [group]
    moments = jnp.concatenate([moments, spread])
    merge = merge_moments(frames)
    moments = along(moments, merge)
    moments, held = tie((moments, held))
    group = swap(held[1])
    moments_one = across(moments, merge)
    gains_one, gains_two = moments_one[3:6], moments_one[6:9]
    moments_one = moments_one[:3]
    every = [(0, z_one.shape[1] // LANES)]
    states_one, (h_one,) = forward(
        z_one, moments_one, gains_one, keep, 1, every, total_frames
    )
    z_two, moments = project([h_one], full_two)
    moments, group = tie((moments, group))
    grads.append(group)
    merge = merge_moments(frames)
    moments = along(moments, merge)
    moments, held = tie((moments, held))
    group = swap(held[2])
    moments_two = across(moments, merge)
    states_two, h_two = forward(
        z_two, moments_two, gains_two, keep, narrow, groups_out, total_frames
    )
    h_two, group = tie((h_two, group))
    grads.append(group)

    second = [swap(h_two[0])]
    dpre, sums = backward(grads, groups_in, states_two, z_two, moments_two, gains_two, keep)
    sums, second[0] = tie((sums, second[0]))
    sums = along(sums, add)
    sums, h_two = tie((sums, h_two))
    group = swap(h_two[1])
    sums_two = across(sums, add)
    dz_two, level_two, dh_one = dproject(
        dpre, z_two, moments_two, gains_two, sums_two, full_two, 1, total_frames, 0, frames
    )
    center_one, center_two = moments_one[2:3], moments_two[2:3]
    terms_two = weight_terms(h_one[0], center_two, [dz_two], [level_two])
    terms_two, dh_one, group = tie((terms_two, dh_one, group))
    second.append(group)
    plane_two = lax.psum_scatter(terms_two, "wide", scatter_dimension=0, tiled=True)
    dpre, sums = backward([dh_one], every, states_one, z_one, moments_one, gains_one, keep)
    sums = along(jnp.concatenate([sums, level_two], 0), add)
    sums, h_two = tie((sums, h_two))
    group = swap(h_two[2])
    sums_one = across(sums, add)
    level_two = sums_one[3:, :]
    sums_one = sums_one[:3]
    back = functools.partial(
        dproject, dpre, z_one, moments_one, gains_one, sums_one, full_one, narrow, total_frames
    )
    dz_early, level_early, da_early = back(0, split)
    da_early, group = tie((da_early, group))
    second.append(group)
    da_early = swap(da_early)
    dz_late, level_late, da_late = back(split, frames)
    terms_one = weight_terms(source, center_one, [dz_early, dz_late], [level_early, level_late])
    da_early, da_late, terms_one, plane_two = tie((da_early, da_late, terms_one, plane_two))
    plane_one = lax.psum_scatter(terms_one, "wide", scatter_dimension=0, tiled=True)
    da_late = swap(da_late)
    level_one = across(level_early + level_late, add)

    whole_two = jnp.concatenate(second, axis=2).reshape(inputs.shape).astype(jnp.float32)
    output = (inputs.astype(jnp.float32) + whole_two).astype(jnp.bfloat16)

    def summed(plane):
        blocks = plane.reshape(plane.shape[0], narrow, part)
        weight = lax.dynamic_index_in_dim(blocks, n, 1, keepdims=False).astype(jnp.float32)
        for k in range(1, narrow):
            block = lax.dynamic_index_in_dim(blocks, n ^ k, 1, keepdims=False)
            weight += lax.ppermute(block, "narrow", [(i, i ^ k) for i in range(narrow)])
        return weight

    span = plane_one.shape[0]
    dw_two = summed(plane_two)
    level_one, da_late = tie((level_one, da_late))
    arrived = jnp.concatenate([da_early, da_late], axis=1).reshape(inputs.shape)
    grad_inputs = cotangent.astype(jnp.float32) + arrived.astype(jnp.float32)
    level_one = along(level_one, add)
    dw_one = summed(plane_one)

    def restored(weight, center, level):
        rows_of = lax.dynamic_slice_in_dim(center, w * span, span, 1).reshape(span, 1)
        return weight + rows_of * lax.dynamic_slice_in_dim(level, n * part, part, 1)

    dw_one = restored(dw_one, center_one, level_one)
    dw_two = restored(dw_two, center_two, level_two)

    def small(sums, moments):
        rstd = lax.rsqrt(moments[1] / total_frames + EPSILON)
        whole_ones = (sums[1] * rstd, sums[0], sums[2])
        return [lax.dynamic_slice_in_dim(v, (n * wide + w) * each, each, 0) for v in whole_ones]

    return (
        output,
        grad_inputs,
        dw_one,
        *small(sums_one, moments_one),
        dw_two,
        *small(sums_two, moments_two),
    )


def solution(mesh):
    neurons = P(("narrow", "wide"))
    frames = P("wide", "narrow")
    weight = P(None, "narrow")
    small = (neurons, neurons, neurons)
    return jax.shard_map(
        functools.partial(per_device, dict(mesh.shape)),
        mesh=mesh,
        in_specs=(frames, P(), weight, *small, weight, *small, frames),
        out_specs=(frames, frames, frames, *small, frames, *small),
        check_vma=False,
    )
```

```python
import functools
import math

import jax
import jax.numpy as jnp
from jax import lax
from jax.experimental import pallas as pl
from jax.experimental.pallas import tpu as pltpu
from jax.sharding import PartitionSpec as P

ROW_LEN = 512
EPSILON = 1e-05
LOG2E = 1.4426950408889634
LN2 = 0.6931471805599453
LANES = 128
SUB = 16
CHUNK = 64
VMEM_LIMIT = 56 * 2**20
BOTH = ("narrow", "wide")

params_of = functools.partial(pltpu.CompilerParams, vmem_limit_bytes=VMEM_LIMIT)
SMEM = pl.BlockSpec(memory_space=pltpu.SMEM)
BRIEF = pl.CostEstimate(flops=1, bytes_accessed=1, transcendentals=0)


def whole(shape):
    return pl.BlockSpec(shape, lambda *_: (0,) * len(shape))


def swap(blocks):
    return lax.all_to_all(blocks, "narrow", split_axis=0, concat_axis=0)


def merge_all(value, merge, axis, size):
    k = size
    while k > 1:
        if k % 4 == 0:
            k //= 4
            turns = (k, 2 * k, 3 * k)
        else:
            k //= 2
            turns = (k,)
        others = [lax.ppermute(value, axis, [(i, i ^ t) for i in range(size)]) for t in turns]
        value = merge([value, *others])
    return value


def add(values):
    while len(values) > 1:
        values = [a + b for a, b in zip(values[::2], values[1::2], strict=True)]
    return values[0]


def merge_moments(frames):
    count = [frames]

    def merge(values):
        summed = add(values)
        row = lax.broadcasted_iota(jnp.int32, summed.shape, 0)
        part = 1 / len(values)
        mean = summed[0:1] * part
        gaps = [v[0:1] - mean for v in values]
        squares = add([gap * gap for gap in gaps]) * count[0]
        count[0] *= len(values)
        scale = jnp.where((row == 0) | (row == 2), part, 1.0)
        return summed * scale + jnp.where(row == 1, squares, 0.0)

    return merge


def gather_rows(weights, wide):
    rows = weights[0].shape[0] // wide
    first = lax.axis_index("wide") * rows
    shares = [lax.dynamic_slice_in_dim(weight, first, rows, 0) for weight in weights]
    return lax.all_gather(jnp.stack(shares), "narrow", axis=1)


def project_kernel(groups, x_refs, w_ref, z_ref, moments_ref, joined_ref=None):
    frames, cols = z_ref.shape
    here = pl.program_id(0)
    step = math.gcd(256, *[x_ref.shape[1] for x_ref in x_refs])
    weight = w_ref[...].reshape(-1, cols)
    sums = jnp.zeros((1, cols), jnp.float32)
    for m in range(0, frames, step):
        acc = None
        for ref, lo, count, feature in groups:
            if not lo <= m < lo + count:
                continue
            x_ref = x_refs[ref]
            block, first, depth = feature
            x = x_ref[block, m - lo : m - lo + step, :]
            term = jnp.dot(x, weight[first : first + depth, :], preferred_element_type=jnp.float32)
            acc = term if acc is None else acc + term
        rounded = acc.astype(jnp.bfloat16)
        z_ref[m : m + step, :] = rounded
        sums += jnp.sum(rounded.astype(jnp.float32), 0, keepdims=True)
    mean = sums / frames
    squares = jnp.zeros((1, cols), jnp.float32)
    for m in range(0, frames, step):
        gap = z_ref[m : m + step, :].astype(jnp.float32) - mean
        squares += jnp.sum(gap * gap, 0, keepdims=True)
    at = pl.ds(pl.multiple_of(here * cols, cols), cols)
    moments_ref[0:1, at] = mean
    moments_ref[1:2, at] = squares
    if joined_ref is None:
        own = x_refs[0][0, :, at].astype(jnp.float32)
        moments_ref[2:3, at] = jnp.sum(own, 0, keepdims=True) / frames
        return
    total = jnp.zeros((1, joined_ref.shape[1]), jnp.float32)
    lo = 0
    for x_ref in x_refs:
        count = x_ref.shape[1]
        own = x_ref[here]
        joined_ref[lo : lo + count, :] = own
        total += jnp.sum(own.astype(jnp.float32), 0, keepdims=True)
        lo += count
    place = pl.ds(pl.multiple_of(here * joined_ref.shape[1], joined_ref.shape[1]), joined_ref.shape[1])
    moments_ref[2:3, place] = total / frames


def project(pieces, weight):
    blocks, _, depth = pieces[0].shape
    frames = sum(p.shape[1] for p in pieces)
    row_blocks, steps, span, width = weight.shape
    rows, cols = row_blocks * span, steps * width
    joined = blocks > 1
    groups = []
    lo = 0
    for i, p in enumerate(pieces):
        groups += [(i, lo, p.shape[1], (k, k * depth, depth)) for k in range(blocks)]
        lo += p.shape[1]
    out_shape = [
        jax.ShapeDtypeStruct((frames, cols), jnp.bfloat16),
        jax.ShapeDtypeStruct((3, cols), jnp.float32),
    ]
    out_specs = [pl.BlockSpec((frames, width), lambda i: (0, i)), whole((3, cols))]
    if joined:
        out_shape.append(jax.ShapeDtypeStruct((frames, rows), jnp.bfloat16))
        out_specs.append(pl.BlockSpec((frames, depth), lambda i: (0, i)))

    def kernel(*refs):
        project_kernel(groups, refs[: len(pieces)], *refs[len(pieces) :])

    return pl.pallas_call(
        kernel,
        grid=(steps,),
        in_specs=[whole(p.shape) for p in pieces]
        + [pl.BlockSpec((row_blocks, 1, span, width), lambda i: (0, i, 0, 0))],
        out_specs=out_specs,
        out_shape=out_shape,
        compiler_params=params_of(),
        cost_estimate=BRIEF,
        name="project",
    )(*pieces, weight)


def to_steps(row_ref, lanes_ref, tiles):
    for j in range(tiles):
        lanes_ref[j : j + 1, :] = row_ref[:, j * LANES : (j + 1) * LANES]


def forward_kernel(total_frames, ranges, keep, moments, gains, z_ref, s_ref, *refs):
    parts = len(ranges)
    h_refs, (vec, state, seq) = refs[:parts], refs[parts:]
    rows, chunk, width = z_ref.shape
    tiles = width // LANES

    @pl.when(pl.program_id(0) == 0)
    def _():
        scale = gains[0:1, :] * lax.rsqrt(moments[1:2, :] / total_frames + EPSILON)
        lanes = [moments[0:1, :], scale * LOG2E, gains[1:2, :] * LOG2E, gains[2:3, :] * LOG2E]
        for i, row in enumerate(lanes):
            for j in range(tiles):
                vec[i, j : j + 1, :] = row[:, j * LANES : (j + 1) * LANES]
        state[...] = jnp.zeros_like(state)

    mean, scale, shift, decay = (vec[i] for i in range(4))
    first = pl.program_id(0) * chunk

    def block(c, running):
        running = list(running)
        for r in range(rows):
            values = z_ref[r, pl.ds(pl.multiple_of(c * SUB, SUB), SUB), :].astype(jnp.float32)
            for j in range(tiles):
                for half in range(SUB // 8):
                    seq[r, pl.ds(half * 8 * tiles + j, 8, stride=tiles), :] = values[
                        half * 8 : half * 8 + 8, j * LANES : (j + 1) * LANES
                    ]
        for k in range(SUB):
            for r in range(rows):
                value = (seq[r, k * tiles : (k + 1) * tiles, :] - mean) * scale + shift
                before = value + (decay * keep[r, first + c * SUB + k]) * running[r]
                fresh = jnp.where(
                    before > 30.0, before * LN2, jnp.log(1.0 + jnp.exp2(before))
                )
                running[r] = fresh
                s_ref[r, pl.ds(pl.multiple_of((c * SUB + k) * tiles, tiles), tiles), :] = fresh
        for (lo, hi, first_row, count), h_ref in zip(ranges, h_refs, strict=True):
            for r in range(first_row, first_row + count):
                per_block = tiles // h_ref.shape[0]
                for q in range(h_ref.shape[0]):
                    for j in range(lo, hi):
                        tile = q * per_block + j
                        halves = [
                            s_ref[
                                r,
                                pl.ds((c * SUB + half * 8) * tiles + tile, 8, stride=tiles),
                                :,
                            ]
                            for half in range(SUB // 8)
                        ]
                        h_ref[
                            q,
                            r - first_row,
                            pl.ds(pl.multiple_of(c * SUB, SUB), SUB),
                            (j - lo) * LANES : (j - lo + 1) * LANES,
                        ] = jnp.concatenate(halves, 0).astype(jnp.bfloat16)
        return tuple(running)

    running = lax.fori_loop(0, chunk // SUB, block, tuple(state[r] for r in range(rows)))
    for r in range(rows):
        state[r] = running[r]


def forward(z, moments, gains, keep, blocks, ranges, total_frames):
    rows, length = keep.shape
    width = z.shape[1]
    tiles = width // LANES
    results = pl.pallas_call(
        functools.partial(forward_kernel, total_frames, ranges),
        grid=(length // CHUNK,),
        in_specs=[
            SMEM,
            whole((3, width)),
            whole((3, width)),
            pl.BlockSpec((rows, CHUNK, width), lambda i: (0, i, 0)),
        ],
        out_specs=[pl.BlockSpec((rows, CHUNK * tiles, LANES), lambda i: (0, i, 0))]
        + [
            pl.BlockSpec((blocks, count, CHUNK, (hi - lo) * LANES), lambda i: (0, 0, i, 0))
            for lo, hi, _, count in ranges
        ],
        out_shape=[jax.ShapeDtypeStruct((rows, length * tiles, LANES), jnp.float32)]
        + [
            jax.ShapeDtypeStruct((blocks, count, length, (hi - lo) * LANES), jnp.bfloat16)
            for lo, hi, _, count in ranges
        ],
        scratch_shapes=[
            pltpu.VMEM((4, tiles, LANES), jnp.float32),
            pltpu.VMEM((rows, tiles, LANES), jnp.float32),
            pltpu.VMEM((rows, SUB * tiles, LANES), jnp.float32),
        ],
        compiler_params=params_of(),
        cost_estimate=BRIEF,
        name="forward",
    )(keep, moments, gains, z.reshape(rows, length, width))
    return results[0], [h.reshape(blocks, h.shape[1] * length, -1) for h in results[1:]]


def backward_kernel(ranges, keep, moments, gains, s_ref, before_ref, z_ref, *refs):
    parts = len(ranges)
    g_refs, (dpre_ref, sums_ref, vec, state, seq, grads) = refs[:parts], refs[parts:]
    rows, chunk, width = z_ref.shape
    tiles = width // LANES
    step = pl.program_id(0)
    first = (pl.num_programs(0) - 1 - step) * chunk

    @pl.when(step == 0)
    def _():
        for j in range(tiles):
            vec[j : j + 1, :] = gains[2:3, j * LANES : (j + 1) * LANES]
        state[...] = jnp.zeros_like(state)
        sums_ref[...] = jnp.zeros_like(sums_ref)

    decay = vec[...]
    mean = moments[0:1, :]
    blocks = chunk // SUB

    def block(i, running):
        *running, dsum = running
        c = blocks - 1 - i
        base = pl.multiple_of(c * SUB, SUB)
        for r in range(rows):
            for (lo, hi), g_ref in zip(ranges, g_refs, strict=True):
                per_block = tiles // g_ref.shape[0]
                for q in range(g_ref.shape[0]):
                    values = g_ref[q, r, pl.ds(base, SUB), :].astype(jnp.float32)
                    for j in range(lo, hi):
                        tile = q * per_block + j
                        for half in range(SUB // 8):
                            seq[r, pl.ds(half * 8 * tiles + tile, 8, stride=tiles), :] = values[
                                half * 8 : half * 8 + 8, (j - lo) * LANES : (j - lo + 1) * LANES
                            ]
        for k in range(SUB - 1, -1, -1):
            for r in range(rows):
                at = c * SUB + k
                s = s_ref[r, pl.ds(pl.multiple_of(at * tiles, tiles), tiles), :]
                if k > 0:
                    prior = s_ref[r, pl.ds(pl.multiple_of((at - 1) * tiles, tiles), tiles), :]
                else:
                    inner = s_ref[
                        r, pl.ds(pl.multiple_of(jnp.maximum(at - 1, 0) * tiles, tiles), tiles), :
                    ]
                    prior = jnp.where(c > 0, inner, before_ref[r])
                mark = keep[r, first + at]
                slope = 1.0 - jnp.exp2(s * -LOG2E)
                dpre = (seq[r, k * tiles : (k + 1) * tiles, :] + running[r]) * slope
                held = dpre * mark
                running[r] = held * decay
                dsum = dsum + held * prior
                grads[r, k * tiles : (k + 1) * tiles, :] = dpre
        gb = jnp.zeros((8, width), jnp.float32)
        gg = jnp.zeros((8, width), jnp.float32)
        for r in range(rows):
            gaps = z_ref[r, pl.ds(base, SUB), :].astype(jnp.float32) - mean
            for half in range(SUB // 8):
                dpre = jnp.concatenate(
                    [
                        grads[r, pl.ds(half * 8 * tiles + j, 8, stride=tiles), :]
                        for j in range(tiles)
                    ],
                    1,
                )
                dpre_ref[r, pl.ds(pl.multiple_of(base + half * 8, 8), 8), :] = dpre
                gb += dpre
                gg += dpre * gaps[half * 8 : half * 8 + 8, :]
        sums_ref[0:8, :] += gb
        sums_ref[8:16, :] += gg
        return (*running, dsum)

    start = tuple(state[r] for r in range(rows)) + (state[rows],)
    *running, dsum = lax.fori_loop(0, blocks, block, start)
    for r in range(rows):
        state[r] = running[r]
    state[rows] = dsum

    @pl.when(step == pl.num_programs(0) - 1)
    def _():
        gb = jnp.sum(sums_ref[0:8, :], 0, keepdims=True)
        gg = jnp.sum(sums_ref[8:16, :], 0, keepdims=True)
        sums_ref[0:1, :] = gb
        sums_ref[1:2, :] = gg
        for j in range(tiles):
            sums_ref[2:3, j * LANES : (j + 1) * LANES] = state[rows, j : j + 1, :]


def backward(grads, ranges, states, z, moments, gains, keep):
    rows, length = keep.shape
    width = z.shape[1]
    tiles = width // LANES
    blocks = grads[0].shape[0]
    last = length // CHUNK - 1
    dpre, sums = pl.pallas_call(
        functools.partial(backward_kernel, ranges),
        grid=(length // CHUNK,),
        in_specs=[
            SMEM,
            whole((3, width)),
            whole((3, width)),
            pl.BlockSpec((rows, CHUNK * tiles, LANES), lambda i: (0, last - i, 0)),
            pl.BlockSpec(
                (rows, tiles, LANES), lambda i: (0, jnp.maximum((last - i) * CHUNK - 1, 0), 0)
            ),
            pl.BlockSpec((rows, CHUNK, width), lambda i: (0, last - i, 0)),
        ]
        + [
            pl.BlockSpec((blocks, rows, CHUNK, (hi - lo) * LANES), lambda i: (0, 0, last - i, 0))
            for lo, hi in ranges
        ],
        out_specs=[
            pl.BlockSpec((rows, CHUNK, width), lambda i: (0, last - i, 0)),
            whole((16, width)),
        ],
        out_shape=[
            jax.ShapeDtypeStruct((rows, length, width), jnp.float32),
            jax.ShapeDtypeStruct((16, width), jnp.float32),
        ],
        scratch_shapes=[
            pltpu.VMEM((tiles, LANES), jnp.float32),
            pltpu.VMEM((rows + 1, tiles, LANES), jnp.float32),
            pltpu.VMEM((rows, SUB * tiles, LANES), jnp.float32),
            pltpu.VMEM((rows, SUB * tiles, LANES), jnp.float32),
        ],
        compiler_params=params_of(),
        cost_estimate=BRIEF,
        name="backward",
    )(
        keep,
        moments,
        gains,
        states,
        states,
        z.reshape(rows, length, width),
        *[g.reshape(blocks, rows, length, -1) for g in grads],
    )
    return dpre.reshape(rows * length, width), sums[0:3]


def dproject_kernel(total_frames, moments, gains, sums, dpre_ref, z_ref, w_ref, *refs):
    dz_ref, level_ref, da_ref, dz_held, weight, arrived = refs
    here = pl.program_id(0)
    last = pl.num_programs(0) - 1
    width = dpre_ref.shape[1]
    slot = lax.rem(here, 2)

    def fetch(j):
        cols = w_ref.shape[3]
        return pltpu.make_async_copy(
            w_ref.at[:, j], weight.at[:, :, pl.ds(j * cols, cols)], arrived.at[j]
        )

    def differentiate():
        rstd = lax.rsqrt(moments[1:2, :] / total_frames + EPSILON)
        scale = gains[0:1, :] * rstd
        level = sums[0:1, :] / total_frames
        slope = sums[1:2, :] * (rstd * rstd) / total_frames
        gap = z_ref[...].astype(jnp.float32) - moments[0:1, :]
        dz = (scale * (dpre_ref[...] - level - gap * slope)).astype(jnp.bfloat16)
        dz_ref[...] = dz
        dz_held[slot] = dz
        level_ref[...] += jnp.sum(dz.astype(jnp.float32), 0, keepdims=True)

    def multiply(da_ref):
        parts = da_ref.shape[0]
        whole_weight = weight[...].reshape(-1, width)
        depth = whole_weight.shape[0] // parts
        for p in range(parts):
            da_ref[p] = lax.dot_general(
                dz_held[1 - slot],
                whole_weight[p * depth : (p + 1) * depth, :],
                (((1,), (1,)), ((), ())),
                preferred_element_type=jnp.float32,
            ).astype(jnp.bfloat16)

    @pl.when(here == 0)
    def _():
        for j in range(w_ref.shape[1]):
            fetch(j).start()
        level_ref[...] = jnp.zeros_like(level_ref)
        differentiate()
        for j in range(w_ref.shape[1]):
            fetch(j).wait()

    @pl.when((here > 0) & (here < last))
    def _():
        multiply(da_ref)
        differentiate()

    @pl.when(here == last)
    def _():
        multiply(da_ref)


def dproject(dpre, z, moments, gains, sums, weight, parts, total_frames, lo, hi):
    frames, width = hi - lo, z.shape[1]
    row_blocks, col_blocks, span, cols = weight.shape
    rows = row_blocks * span
    step = math.gcd(frames, 256)
    steps = frames // step
    return pl.pallas_call(
        functools.partial(dproject_kernel, total_frames),
        grid=(steps + 1,),
        in_specs=[
            whole((3, width)),
            whole((3, width)),
            whole((3, width)),
            pl.BlockSpec((step, width), lambda i: (jnp.minimum(i, steps - 1) + lo // step, 0)),
            pl.BlockSpec((step, width), lambda i: (jnp.minimum(i, steps - 1) + lo // step, 0)),
            pl.BlockSpec(memory_space=pl.ANY),
        ],
        out_specs=[
            pl.BlockSpec((step, width), lambda i: (jnp.minimum(i, steps - 1), 0)),
            whole((1, width)),
            pl.BlockSpec(
                (parts, step, rows // parts), lambda i: (0, jnp.maximum(i - 1, 0), 0)
            ),
        ],
        out_shape=[
            jax.ShapeDtypeStruct((frames, width), jnp.bfloat16),
            jax.ShapeDtypeStruct((1, width), jnp.float32),
            jax.ShapeDtypeStruct((parts, frames, rows // parts), jnp.bfloat16),
        ],
        scratch_shapes=[
            pltpu.VMEM((2, step, width), jnp.bfloat16),
            pltpu.VMEM((row_blocks, span, width), jnp.bfloat16),
            pltpu.SemaphoreType.DMA((col_blocks,)),
        ],
        compiler_params=params_of(),
        cost_estimate=BRIEF,
        name="dproject",
    )(moments, gains, sums, dpre, z, weight)


def weight_kernel(pieces, *refs):
    level_refs, dz_refs = refs[:pieces], refs[pieces : 2 * pieces]
    center_ref, source_ref, out_ref = refs[2 * pieces :]
    level = sum(level_ref[...] for level_ref in level_refs)
    center = jnp.transpose(jnp.broadcast_to(center_ref[...], (8, center_ref.shape[1])))[:, :1]
    terms = -center * level
    lo = 0
    for dz_ref in dz_refs:
        count = dz_ref.shape[0]
        terms += lax.dot_general(
            source_ref[lo : lo + count, :],
            dz_ref[...],
            (((0,), (0,)), ((), ())),
            preferred_element_type=jnp.float32,
        )
        lo += count
    out_ref[...] = terms.astype(jnp.bfloat16)


def weight_terms(source, center, dz, levels):
    frames, rows = source.shape
    cols = dz[0].shape[1]
    tile = 512
    return pl.pallas_call(
        functools.partial(weight_kernel, len(dz)),
        grid=(rows // tile,),
        in_specs=[whole((1, cols))] * len(dz)
        + [whole(d.shape) for d in dz]
        + [
            pl.BlockSpec((1, tile), lambda i: (0, i)),
            pl.BlockSpec((frames, tile), lambda i: (0, i)),
        ],
        out_specs=pl.BlockSpec((tile, cols), lambda i: (i, 0)),
        out_shape=jax.ShapeDtypeStruct((rows, cols), jnp.bfloat16),
        compiler_params=params_of(),
        cost_estimate=BRIEF,
        name="weight",
    )(*levels, *dz, center, source)


def per_device(sizes, inputs, flags, w_one, *rest):
    gamma_one, beta_one, decay_one, w_two, gamma_two, beta_two, decay_two, cotangent = rest
    wide, narrow = sizes["wide"], sizes["narrow"]
    n = lax.axis_index("narrow")
    w = lax.axis_index("wide")
    frames = inputs.shape[0] // narrow
    part = inputs.shape[1]
    tiles = part // LANES
    total_frames = inputs.shape[0] * wide
    rows = frames // ROW_LEN
    first = w * inputs.shape[0] + n * frames
    keep = lax.dynamic_slice_in_dim(flags, first, frames, 0).reshape(rows, ROW_LEN)
    keep = (1 - keep).astype(jnp.float32)
    tie = lax.optimization_barrier

    def along(value, merge):
        return merge_all(value, merge, "narrow", narrow)

    def across(value, merge):
        return merge_all(value, merge, "wide", wide)

    own = jnp.stack([gamma_one, beta_one, decay_one, gamma_two, beta_two, decay_two])
    each = own.shape[1]
    spread = jnp.zeros((6, each * wide * narrow), jnp.float32)
    spread = lax.dynamic_update_slice_in_dim(spread, own, (n * wide + w) * each, 1)

    groups_in = [(0, tiles // 4), (tiles // 4, 3 * tiles // 4), (3 * tiles // 4, tiles)]
    groups_out = [(lo, hi, 0, rows) for lo, hi in groups_in[:2]]
    groups_out += [(*groups_in[2], 0, rows // 2), (*groups_in[2], rows // 2, rows // 2)]

    held = [
        cotangent[:, lo * LANES : hi * LANES].reshape(narrow, frames, -1) for lo, hi in groups_in
    ]

    split = frames // 4
    blocks = inputs.reshape(narrow, frames, part)
    early, late = blocks[:, :split], blocks[:, split:]
    early = swap(early)
    shares = gather_rows([w_one, w_two], wide)
    shares, early, late, held, spread = tie((shares, early, late, held, spread))
    late = swap(late)
    gains = along(across(spread, add), add)
    share_one, share_two = shares[0], shares[1]
    full_one = lax.all_gather(share_one, "wide", axis=0)
    late, held, share_two, gains = tie((late, held, share_two, gains))
    gains_one, gains_two = gains[:3], gains[3:]
    full_two = lax.all_gather(share_two, "wide", axis=0)
    group = swap(held[0])
    z_one, moments, source = project([early, late], full_one)
    moments, group = tie((moments, group))
    grads = [group]
    merge = merge_moments(frames)
    moments = along(moments, merge)
    moments, held = tie((moments, held))
    group = swap(held[1])
    moments_one = across(moments, merge)
    every = [(0, z_one.shape[1] // LANES)]
    states_one, (h_one,) = forward(
        z_one, moments_one, gains_one, keep, 1, [(*every[0], 0, rows)], total_frames
    )
    z_two, moments = project([h_one], full_two)
    moments, group = tie((moments, group))
    grads.append(group)
    merge = merge_moments(frames)
    moments = along(moments, merge)
    moments, held = tie((moments, held))
    group = swap(held[2])
    moments_two = across(moments, merge)
    states_two, h_two = forward(
        z_two, moments_two, gains_two, keep, narrow, groups_out, total_frames
    )
    h_two, group = tie((h_two, group))
    grads.append(group)

    second = [swap(h_two[0])]
    dpre, sums = backward(grads, groups_in, states_two, z_two, moments_two, gains_two, keep)
    sums, second[0] = tie((sums, second[0]))
    sums = along(sums, add)
    sums, h_two = tie((sums, h_two))
    group = swap(h_two[1])
    sums_two = across(sums, add)
    dz_two, level_two, dh_one = dproject(
        dpre, z_two, moments_two, gains_two, sums_two, full_two, 1, total_frames, 0, frames
    )
    center_one, center_two = moments_one[2:3], moments_two[2:3]
    terms_two = weight_terms(h_one[0], center_two, [dz_two], [level_two])
    terms_two, dh_one, group = tie((terms_two, dh_one, group))
    second.append(group)
    plane_two = lax.psum_scatter(terms_two, "wide", scatter_dimension=0, tiled=True)
    group = swap(h_two[2])
    dpre, sums = backward([dh_one], every, states_one, z_one, moments_one, gains_one, keep)
    sums, group = tie((sums, group))
    thirds = [group]
    sums = along(jnp.concatenate([sums, level_two], 0), add)
    sums, h_two = tie((sums, h_two))
    group = swap(h_two[3])
    sums_one = across(sums, add)
    level_two = sums_one[3:, :]
    sums_one = sums_one[:3]
    back = functools.partial(
        dproject, dpre, z_one, moments_one, gains_one, sums_one, full_one, narrow, total_frames
    )
    split = frames // 2
    dz_early, level_early, da_early = back(0, split)
    da_early, group = tie((da_early, group))
    thirds.append(group)
    second.append(jnp.concatenate(thirds, 1))
    da_early = swap(da_early)
    dz_late, level_late, da_late = back(split, frames)
    terms_one = weight_terms(source, center_one, [dz_early, dz_late], [level_early, level_late])
    da_early, da_late, terms_one, plane_two = tie((da_early, da_late, terms_one, plane_two))
    plane_one = lax.psum_scatter(terms_one, "wide", scatter_dimension=0, tiled=True)
    da_late = swap(da_late)
    level_one = level_early + level_late
    level_one = across(level_one, add)

    whole_two = jnp.concatenate(second, axis=2).reshape(inputs.shape).astype(jnp.float32)
    output = (inputs.astype(jnp.float32) + whole_two).astype(jnp.bfloat16)

    span = plane_one.shape[0]
    blocks = plane_two.reshape(span, narrow, part)
    mine = lax.dynamic_index_in_dim(blocks, n, 1, keepdims=False)
    others = [
        lax.ppermute(
            lax.dynamic_index_in_dim(blocks, n ^ k, 1, keepdims=False),
            "narrow",
            [(i, i ^ k) for i in range(narrow)],
        )
        for k in range(1, narrow)
    ]
    level_one, da_late = tie((level_one, da_late))
    arrived = jnp.concatenate([da_early, da_late], axis=1).reshape(inputs.shape)
    grad_inputs = cotangent.astype(jnp.float32) + arrived.astype(jnp.float32)
    blocks = swap(plane_one.reshape(span, narrow, part).transpose(1, 0, 2))
    for k in (1, 2):
        level_one = level_one + lax.ppermute(
            level_one, "narrow", [(i, i ^ k) for i in range(narrow)]
        )
    mine, others, blocks = tie((mine, others, blocks))
    dw_two = mine.astype(jnp.float32) + sum(other.astype(jnp.float32) for other in others)
    dw_one = jnp.sum(blocks.astype(jnp.float32), 0)

    def restored(weight, center, level):
        rows_of = lax.dynamic_slice_in_dim(center, w * span, span, 1).reshape(span, 1)
        return weight + rows_of * lax.dynamic_slice_in_dim(level, n * part, part, 1)

    dw_one = restored(dw_one, center_one, level_one)
    dw_two = restored(dw_two, center_two, level_two)

    def small(sums, moments):
        rstd = lax.rsqrt(moments[1] / total_frames + EPSILON)
        whole_ones = (sums[1] * rstd, sums[0], sums[2])
        return [lax.dynamic_slice_in_dim(v, (n * wide + w) * each, each, 0) for v in whole_ones]

    return (
        output,
        grad_inputs,
        dw_one,
        *small(sums_one, moments_one),
        dw_two,
        *small(sums_two, moments_two),
    )


def solution(mesh):
    neurons = P(("narrow", "wide"))
    frames = P("wide", "narrow")
    weight = P(None, "narrow")
    small = (neurons, neurons, neurons)
    return jax.shard_map(
        functools.partial(per_device, dict(mesh.shape)),
        mesh=mesh,
        in_specs=(frames, P(), weight, *small, weight, *small, frames),
        out_specs=(frames, frames, frames, *small, frames, *small),
        check_vma=False,
    )
```

```python
import functools
import math

import jax
import jax.numpy as jnp
from jax import lax
from jax.experimental import pallas as pl
from jax.experimental.pallas import tpu as pltpu
from jax.sharding import PartitionSpec as P

ROW_LEN = 512
EPSILON = 1e-05
LOG2E = 1.4426950408889634
LN2 = 0.6931471805599453
LANES = 128
SUB = 16
CHUNK = 64
VMEM_LIMIT = 56 * 2**20
BOTH = ("narrow", "wide")

params_of = functools.partial(pltpu.CompilerParams, vmem_limit_bytes=VMEM_LIMIT)
SMEM = pl.BlockSpec(memory_space=pltpu.SMEM)
BRIEF = pl.CostEstimate(flops=1, bytes_accessed=1, transcendentals=0)


def whole(shape):
    return pl.BlockSpec(shape, lambda *_: (0,) * len(shape))


def merge_all(value, merge, axis, size, open_end=False):
    k = size
    while k > 1:
        if open_end and k == 2:
            return [value, lax.ppermute(value, axis, [(i, i ^ 1) for i in range(size)])]
        if k % 4 == 0 and not (open_end and k == 4):
            k //= 4
            turns = (k, 2 * k, 3 * k)
        else:
            k //= 2
            turns = (k,)
        others = [lax.ppermute(value, axis, [(i, i ^ t) for i in range(size)]) for t in turns]
        value = merge([value, *others])
    return value


def add(values):
    while len(values) > 1:
        values = [a + b for a, b in zip(values[::2], values[1::2], strict=True)]
    return values[0]


def merge_moments(frames):
    count = [frames]

    def merge(values):
        summed = add(values)
        row = lax.broadcasted_iota(jnp.int32, summed.shape, 0)
        part = 1 / len(values)
        mean = summed[0:1] * part
        gaps = [v[0:1] - mean for v in values]
        squares = add([gap * gap for gap in gaps]) * count[0]
        count[0] *= len(values)
        scale = jnp.where((row == 0) | (row == 2), part, 1.0)
        return summed * scale + jnp.where(row == 1, squares, 0.0)

    return merge


def gather_rows(weights, wide):
    rows = weights[0].shape[0] // wide
    first = lax.axis_index("wide") * rows
    shares = [lax.dynamic_slice_in_dim(weight, first, rows, 0) for weight in weights]
    return lax.all_gather(jnp.stack(shares), "narrow", axis=1)


def project_kernel(blocks, cuts, order, *refs):
    pieces = len(cuts) - 1
    x_refs = [refs[i * blocks : (i + 1) * blocks] for i in range(pieces)]
    w_ref, z_ref, moments_ref, *joined_ref = refs[pieces * blocks :]
    frames, cols = z_ref.shape
    depth = x_refs[0][0].shape[1]
    here = pl.program_id(0)
    step = math.gcd(256, *cuts)
    per_block = w_ref.shape[0] // blocks
    weights = [
        w_ref[pl.ds(order[k] * per_block, per_block)].reshape(depth, cols) for k in range(blocks)
    ]
    sums = jnp.zeros((1, cols), jnp.float32)
    for piece in range(pieces):
        for m in range(cuts[piece], cuts[piece + 1], step):
            acc = None
            for x_ref, weight in zip(x_refs[piece], weights, strict=True):
                x = x_ref[m - cuts[piece] : m - cuts[piece] + step, :]
                term = jnp.dot(x, weight, preferred_element_type=jnp.float32)
                acc = term if acc is None else acc + term
            rounded = acc.astype(jnp.bfloat16)
            z_ref[m : m + step, :] = rounded
            sums += jnp.sum(rounded.astype(jnp.float32), 0, keepdims=True)
    mean = sums / frames
    squares = jnp.zeros((1, cols), jnp.float32)
    for m in range(0, frames, step):
        gap = z_ref[m : m + step, :].astype(jnp.float32) - mean
        squares += jnp.sum(gap * gap, 0, keepdims=True)
    at = pl.ds(pl.multiple_of(here * cols, cols), cols)
    moments_ref[0:1, at] = mean
    moments_ref[1:2, at] = squares
    if not joined_ref:
        own = x_refs[0][0][:, at].astype(jnp.float32)
        moments_ref[2:3, at] = jnp.sum(own, 0, keepdims=True) / frames
        return
    for k in range(blocks):

        @pl.when(here == k)
        def _():
            total = jnp.zeros((1, depth), jnp.float32)
            for piece in range(pieces):
                own = x_refs[piece][k][...]
                joined_ref[0][cuts[piece] : cuts[piece + 1], :] = own
                total += jnp.sum(own.astype(jnp.float32), 0, keepdims=True)
            place = pl.ds(pl.multiple_of(order[k] * depth, depth), depth)
            moments_ref[2:3, place] = total / frames


def project(pieces, order, weight):
    blocks = len(pieces[0])
    depth = pieces[0][0].shape[1]
    cuts = [0]
    for piece in pieces:
        cuts.append(cuts[-1] + piece[0].shape[0])
    frames = cuts[-1]
    row_blocks, steps, span, width = weight.shape
    rows, cols = row_blocks * span, steps * width
    out_shape = [
        jax.ShapeDtypeStruct((frames, cols), jnp.bfloat16),
        jax.ShapeDtypeStruct((3, cols), jnp.float32),
    ]
    out_specs = [pl.BlockSpec((frames, width), lambda i, o: (0, i)), whole((3, cols))]
    if blocks > 1:
        out_shape.append(jax.ShapeDtypeStruct((frames, rows), jnp.bfloat16))
        out_specs.append(pl.BlockSpec((frames, depth), lambda i, o: (0, o[i])))
    flat = [block for piece in pieces for block in piece]
    return pl.pallas_call(
        functools.partial(project_kernel, blocks, cuts),
        grid_spec=pltpu.PrefetchScalarGridSpec(
            num_scalar_prefetch=1,
            grid=(steps,),
            in_specs=[whole(block.shape) for block in flat]
            + [pl.BlockSpec((row_blocks, None, span, width), lambda i, o: (0, i, 0, 0))],
            out_specs=out_specs,
        ),
        out_shape=out_shape,
        compiler_params=params_of(),
        cost_estimate=BRIEF,
        name="project",
    )(order, *flat, weight)


def to_steps(row_ref, lanes_ref, tiles):
    for j in range(tiles):
        lanes_ref[j : j + 1, :] = row_ref[:, j * LANES : (j + 1) * LANES]


def forward_kernel(total_frames, groups, order, keep, mine, other, gains, z_ref, s_ref, moments, *refs):
    *h_refs, vec, state, seq = refs
    rows, chunk, width = z_ref.shape
    tiles = width // LANES

    @pl.when(pl.program_id(0) == 0)
    def _():
        gap = mine[0:1, :] - other[0:1, :]
        squares = mine[1:2, :] + other[1:2, :] + gap * gap * (total_frames / 4)
        scale = gains[0:1, :] * lax.rsqrt(squares / total_frames + EPSILON)
        moments[...] = (mine[...] + other[...]) * 0.5
        moments[1:2, :] = squares
        lanes = [moments[0:1, :], scale * LOG2E, gains[1:2, :] * LOG2E, gains[2:3, :] * LOG2E]
        for i, row in enumerate(lanes):
            for j in range(tiles):
                vec[i, j : j + 1, :] = row[:, j * LANES : (j + 1) * LANES]
        state[...] = jnp.zeros_like(state)

    mean, scale, shift, decay = (vec[i] for i in range(4))
    first = pl.program_id(0) * chunk

    def block(c, running):
        running = list(running)
        for r in range(rows):
            values = z_ref[r, pl.ds(pl.multiple_of(c * SUB, SUB), SUB), :].astype(jnp.float32)
            for j in range(tiles):
                for half in range(SUB // 8):
                    seq[r, pl.ds(half * 8 * tiles + j, 8, stride=tiles), :] = values[
                        half * 8 : half * 8 + 8, j * LANES : (j + 1) * LANES
                    ]
        for k in range(SUB):
            for r in range(rows):
                value = (seq[r, k * tiles : (k + 1) * tiles, :] - mean) * scale + shift
                before = value + (decay * keep[r, first + c * SUB + k]) * running[r]
                fresh = jnp.where(
                    before > 30.0, before * LN2, jnp.log(1.0 + jnp.exp2(before))
                )
                running[r] = fresh
                s_ref[r, pl.ds(pl.multiple_of((c * SUB + k) * tiles, tiles), tiles), :] = fresh
        def rounded(r, tile):
            halves = [
                s_ref[r, pl.ds((c * SUB + half * 8) * tiles + tile, 8, stride=tiles), :]
                for half in range(SUB // 8)
            ]
            return jnp.concatenate(halves, 0).astype(jnp.bfloat16)

        place = pl.ds(pl.multiple_of(c * SUB, SUB), SUB)
        left = list(h_refs)
        for kind, units in groups:
            if kind == "rows":
                h_ref = left.pop(0)
                for r in range(rows):
                    for j in range(tiles):
                        h_ref[r, place, j * LANES : (j + 1) * LANES] = rounded(r, j)
            elif kind == "blocks":
                h_ref = left.pop(0)
                per_block = tiles // h_ref.shape[0]
                for q in range(h_ref.shape[0]):
                    for u, (j, r) in enumerate(units):
                        h_ref[q, u, place, :] = rounded(r, q * per_block + j)
            else:
                count = order.shape[0]
                for k in range(count):
                    h_ref = left.pop(0)
                    for u, (j, r) in enumerate(units):
                        h_ref[u, place, :] = rounded(r, order[k] * (tiles // count) + j)
        return tuple(running)

    running = lax.fori_loop(0, chunk // SUB, block, tuple(state[r] for r in range(rows)))
    for r in range(rows):
        state[r] = running[r]


def unit_shapes(groups, blocks, rows, width, length):
    shapes = []
    for kind, units in groups:
        if kind == "rows":
            shapes.append((rows, length, width))
        elif kind == "blocks":
            shapes.append((blocks, len(units), length, LANES))
        else:
            shapes += [(len(units), length, LANES)] * blocks
    return shapes


def unit_spec(shape, at):
    if len(shape) == 3:
        return pl.BlockSpec((shape[0], CHUNK, shape[2]), lambda i: (0, at(i), 0))
    return pl.BlockSpec((*shape[:2], CHUNK, LANES), lambda i: (0, 0, at(i), 0))


def forward(z, moments, gains, keep, order, groups, total_frames):
    rows, length = keep.shape
    width = z.shape[1]
    tiles = width // LANES
    shapes = unit_shapes(groups, order.shape[0], rows, width, length)
    states, merged, *results = pl.pallas_call(
        functools.partial(forward_kernel, total_frames, groups),
        grid=(length // CHUNK,),
        in_specs=[
            SMEM,
            SMEM,
            whole((3, width)),
            whole((3, width)),
            whole((3, width)),
            pl.BlockSpec((rows, CHUNK, width), lambda i: (0, i, 0)),
        ],
        out_specs=[
            pl.BlockSpec((rows, CHUNK * tiles, LANES), lambda i: (0, i, 0)),
            whole((3, width)),
        ]
        + [unit_spec(shape, lambda i: i) for shape in shapes],
        out_shape=[
            jax.ShapeDtypeStruct((rows, length * tiles, LANES), jnp.float32),
            jax.ShapeDtypeStruct((3, width), jnp.float32),
        ]
        + [jax.ShapeDtypeStruct(shape, jnp.bfloat16) for shape in shapes],
        scratch_shapes=[
            pltpu.VMEM((4, tiles, LANES), jnp.float32),
            pltpu.VMEM((rows, tiles, LANES), jnp.float32),
            pltpu.VMEM((rows, SUB * tiles, LANES), jnp.float32),
        ],
        compiler_params=params_of(),
        cost_estimate=BRIEF,
        name="forward",
    )(order, keep, *moments, gains, z.reshape(rows, length, width))
    grouped = []
    for kind, _ in groups:
        grouped.append([results.pop(0) for _ in range(order.shape[0] if kind == "line" else 1)])
    return states, merged, grouped


def backward_kernel(groups, order, keep, moments, gains, extra, s_ref, before_ref, z_ref, *refs):
    *g_refs, dpre_ref, out_ref, sums_ref, vec, state, seq, grads = refs
    rows, chunk, width = z_ref.shape
    tiles = width // LANES
    step = pl.program_id(0)
    first = (pl.num_programs(0) - 1 - step) * chunk

    @pl.when(step == 0)
    def _():
        for j in range(tiles):
            vec[j : j + 1, :] = gains[2:3, j * LANES : (j + 1) * LANES]
        state[...] = jnp.zeros_like(state)
        sums_ref[...] = jnp.zeros_like(sums_ref)

    decay = vec[...]
    mean = moments[0:1, :]
    blocks = chunk // SUB

    def block(i, running):
        *running, dsum = running
        c = blocks - 1 - i
        base = pl.multiple_of(c * SUB, SUB)
        def spread(r, tile, values):
            for half in range(SUB // 8):
                seq[r, pl.ds(half * 8 * tiles + tile, 8, stride=tiles), :] = values[
                    half * 8 : half * 8 + 8, :
                ]

        left = list(g_refs)
        for kind, units in groups:
            if kind == "rows":
                g_ref = left.pop(0)
                for r in range(rows):
                    values = g_ref[r, pl.ds(base, SUB), :].astype(jnp.float32)
                    for j in range(tiles):
                        spread(r, j, values[:, j * LANES : (j + 1) * LANES])
            elif kind == "blocks":
                g_ref = left.pop(0)
                per_block = tiles // g_ref.shape[0]
                for q in range(g_ref.shape[0]):
                    for u, (j, r) in enumerate(units):
                        values = g_ref[q, u, pl.ds(base, SUB), :].astype(jnp.float32)
                        spread(r, q * per_block + j, values)
            else:
                count = order.shape[0]
                for k in range(count):
                    g_ref = left.pop(0)
                    for u, (j, r) in enumerate(units):
                        values = g_ref[u, pl.ds(base, SUB), :].astype(jnp.float32)
                        spread(r, order[k] * (tiles // count) + j, values)
        for k in range(SUB - 1, -1, -1):
            for r in range(rows):
                at = c * SUB + k
                s = s_ref[r, pl.ds(pl.multiple_of(at * tiles, tiles), tiles), :]
                if k > 0:
                    prior = s_ref[r, pl.ds(pl.multiple_of((at - 1) * tiles, tiles), tiles), :]
                else:
                    inner = s_ref[
                        r, pl.ds(pl.multiple_of(jnp.maximum(at - 1, 0) * tiles, tiles), tiles), :
                    ]
                    prior = jnp.where(c > 0, inner, before_ref[r])
                mark = keep[r, first + at]
                slope = 1.0 - jnp.exp2(s * -LOG2E)
                dpre = (seq[r, k * tiles : (k + 1) * tiles, :] + running[r]) * slope
                held = dpre * mark
                running[r] = held * decay
                dsum = dsum + held * prior
                grads[r, k * tiles : (k + 1) * tiles, :] = dpre
        gb = jnp.zeros((8, width), jnp.float32)
        gg = jnp.zeros((8, width), jnp.float32)
        for r in range(rows):
            gaps = z_ref[r, pl.ds(base, SUB), :].astype(jnp.float32) - mean
            for half in range(SUB // 8):
                dpre = jnp.concatenate(
                    [
                        grads[r, pl.ds(half * 8 * tiles + j, 8, stride=tiles), :]
                        for j in range(tiles)
                    ],
                    1,
                )
                dpre_ref[r, pl.ds(pl.multiple_of(base + half * 8, 8), 8), :] = dpre
                gb += dpre
                gg += dpre * gaps[half * 8 : half * 8 + 8, :]
        sums_ref[0:8, :] += gb
        sums_ref[8:16, :] += gg
        return (*running, dsum)

    start = tuple(state[r] for r in range(rows)) + (state[rows],)
    *running, dsum = lax.fori_loop(0, blocks, block, start)
    for r in range(rows):
        state[r] = running[r]
    state[rows] = dsum

    @pl.when(step == pl.num_programs(0) - 1)
    def _():
        gb = jnp.sum(sums_ref[0:8, :], 0, keepdims=True)
        gg = jnp.sum(sums_ref[8:16, :], 0, keepdims=True)
        out_ref[0:1, :] = gb
        out_ref[1:2, :] = gg
        for j in range(tiles):
            out_ref[2:3, j * LANES : (j + 1) * LANES] = state[rows, j : j + 1, :]
        out_ref[3:4, :] = extra[...]


def backward(grads, order, groups, states, z, moments, gains, keep, extra):
    rows, length = keep.shape
    width = z.shape[1]
    tiles = width // LANES
    last = length // CHUNK - 1
    grads = [g for group in grads for g in group]
    dpre, sums = pl.pallas_call(
        functools.partial(backward_kernel, groups),
        grid=(length // CHUNK,),
        in_specs=[
            SMEM,
            SMEM,
            whole((3, width)),
            whole((3, width)),
            whole((1, width)),
            pl.BlockSpec((rows, CHUNK * tiles, LANES), lambda i: (0, last - i, 0)),
            pl.BlockSpec(
                (rows, tiles, LANES), lambda i: (0, jnp.maximum((last - i) * CHUNK - 1, 0), 0)
            ),
            pl.BlockSpec((rows, CHUNK, width), lambda i: (0, last - i, 0)),
        ]
        + [unit_spec(g.shape, lambda i: last - i) for g in grads],
        out_specs=[
            pl.BlockSpec((rows, CHUNK, width), lambda i: (0, last - i, 0)),
            whole((4, width)),
        ],
        out_shape=[
            jax.ShapeDtypeStruct((rows, length, width), jnp.float32),
            jax.ShapeDtypeStruct((4, width), jnp.float32),
        ],
        scratch_shapes=[
            pltpu.VMEM((16, width), jnp.float32),
            pltpu.VMEM((tiles, LANES), jnp.float32),
            pltpu.VMEM((rows + 1, tiles, LANES), jnp.float32),
            pltpu.VMEM((rows, SUB * tiles, LANES), jnp.float32),
            pltpu.VMEM((rows, SUB * tiles, LANES), jnp.float32),
        ],
        compiler_params=params_of(),
        cost_estimate=BRIEF,
        name="backward",
    )(
        order,
        keep,
        moments,
        gains,
        extra,
        states,
        states,
        z.reshape(rows, length, width),
        *grads,
    )
    return dpre.reshape(rows * length, width), sums


def dproject_kernel(total_frames, order, moments, gains, mine, other, dpre_ref, z_ref, w_ref, *refs):
    dz_ref, level_ref, sums_ref, *da_refs, dz_held, weight, arrived = refs
    here = pl.program_id(0)
    last = pl.num_programs(0) - 1
    width = dpre_ref.shape[1]
    slot = lax.rem(here, 2)

    def fetch(j):
        cols = w_ref.shape[3]
        return pltpu.make_async_copy(
            w_ref.at[:, j], weight.at[:, :, pl.ds(j * cols, cols)], arrived.at[j]
        )

    def differentiate():
        rstd = lax.rsqrt(moments[1:2, :] / total_frames + EPSILON)
        scale = gains[0:1, :] * rstd
        level = (mine[0:1, :] + other[0:1, :]) / total_frames
        slope = (mine[1:2, :] + other[1:2, :]) * (rstd * rstd) / total_frames
        gap = z_ref[...].astype(jnp.float32) - moments[0:1, :]
        dz = (scale * (dpre_ref[...] - level - gap * slope)).astype(jnp.bfloat16)
        dz_ref[...] = dz
        dz_held[slot] = dz
        level_ref[...] += jnp.sum(dz.astype(jnp.float32), 0, keepdims=True)

    def multiply():
        per_part = weight.shape[0] // len(da_refs)
        for k, da_ref in enumerate(da_refs):
            part = weight[pl.ds(order[k] * per_part, per_part)].reshape(-1, width)
            da_ref[...] = lax.dot_general(
                dz_held[1 - slot],
                part,
                (((1,), (1,)), ((), ())),
                preferred_element_type=jnp.float32,
            ).astype(jnp.bfloat16)

    @pl.when(here == 0)
    def _():
        for j in range(w_ref.shape[1]):
            fetch(j).start()
        level_ref[...] = jnp.zeros_like(level_ref)
        sums_ref[...] = mine[...] + other[...]
        differentiate()
        for j in range(w_ref.shape[1]):
            fetch(j).wait()

    @pl.when((here > 0) & (here < last))
    def _():
        multiply()
        differentiate()

    @pl.when(here == last)
    def _():
        multiply()


def dproject(dpre, z, moments, gains, sums, weight, order, total_frames, lo, hi):
    frames, width = hi - lo, z.shape[1]
    row_blocks, col_blocks, span, cols = weight.shape
    parts = order.shape[0]
    depth = row_blocks * span // parts
    step = math.gcd(frames, 256)
    steps = frames // step
    dz, level, merged, *da = pl.pallas_call(
        functools.partial(dproject_kernel, total_frames),
        grid=(steps + 1,),
        in_specs=[
            SMEM,
            whole((3, width)),
            whole((3, width)),
            whole((4, width)),
            whole((4, width)),
            pl.BlockSpec((step, width), lambda i: (jnp.minimum(i, steps - 1) + lo // step, 0)),
            pl.BlockSpec((step, width), lambda i: (jnp.minimum(i, steps - 1) + lo // step, 0)),
            pl.BlockSpec(memory_space=pl.ANY),
        ],
        out_specs=[
            pl.BlockSpec((step, width), lambda i: (jnp.minimum(i, steps - 1), 0)),
            whole((1, width)),
            whole((4, width)),
        ]
        + [pl.BlockSpec((step, depth), lambda i: (jnp.maximum(i - 1, 0), 0))] * parts,
        out_shape=[
            jax.ShapeDtypeStruct((frames, width), jnp.bfloat16),
            jax.ShapeDtypeStruct((1, width), jnp.float32),
            jax.ShapeDtypeStruct((4, width), jnp.float32),
        ]
        + [jax.ShapeDtypeStruct((frames, depth), jnp.bfloat16)] * parts,
        scratch_shapes=[
            pltpu.VMEM((2, step, width), jnp.bfloat16),
            pltpu.VMEM((row_blocks, span, width), jnp.bfloat16),
            pltpu.SemaphoreType.DMA((col_blocks,)),
        ],
        compiler_params=params_of(),
        cost_estimate=BRIEF,
        name="dproject",
    )(order, moments, gains, *sums, dpre, z, weight)
    return dz, level, merged, da


def weight_kernel(pieces, *refs):
    level_refs, dz_refs = refs[:pieces], refs[pieces : 2 * pieces]
    center_ref, source_ref, out_ref = refs[2 * pieces :]
    level = sum(level_ref[...] for level_ref in level_refs)
    center = jnp.transpose(jnp.broadcast_to(center_ref[...], (8, center_ref.shape[1])))[:, :1]
    terms = -center * level
    lo = 0
    for dz_ref in dz_refs:
        count = dz_ref.shape[0]
        terms += lax.dot_general(
            source_ref[lo : lo + count, :],
            dz_ref[...],
            (((0,), (0,)), ((), ())),
            preferred_element_type=jnp.float32,
        )
        lo += count
    out_ref[...] = terms.astype(jnp.bfloat16)


def weight_terms(source, center, dz, levels):
    frames, rows = source.shape
    cols = dz[0].shape[1]
    tile = 512
    return pl.pallas_call(
        functools.partial(weight_kernel, len(dz)),
        grid=(rows // tile,),
        in_specs=[whole((1, cols))] * len(dz)
        + [whole(d.shape) for d in dz]
        + [
            pl.BlockSpec((1, tile), lambda i: (0, i)),
            pl.BlockSpec((frames, tile), lambda i: (0, i)),
        ],
        out_specs=pl.BlockSpec((tile, cols), lambda i: (i, 0)),
        out_shape=jax.ShapeDtypeStruct((rows, cols), jnp.bfloat16),
        compiler_params=params_of(),
        cost_estimate=BRIEF,
        name="weight",
    )(*levels, *dz, center, source)


def small_kernel(total_frames, place, *refs):
    ins, outs = refs[:4], refs[4:]
    each = outs[0].shape[1]
    first = place[0] * each
    aligned = pl.multiple_of(first // LANES * LANES, LANES)
    turn = lax.rem(LANES - (first - aligned), LANES)

    def own(ref, row):
        return pltpu.roll(ref[row : row + 1, pl.ds(aligned, LANES)], turn, 1)[:, :each]

    for i in range(2):
        sums, moments = ins[2 * i : 2 * i + 2]
        rstd = lax.rsqrt(own(moments, 1) / total_frames + EPSILON)
        outs[3 * i][...] = own(sums, 1) * rstd
        outs[3 * i + 1][...] = own(sums, 0)
        outs[3 * i + 2][...] = own(sums, 2)


def small_gradients(place, each, total_frames, *values):
    results = pl.pallas_call(
        functools.partial(small_kernel, total_frames),
        in_specs=[SMEM] + [pl.BlockSpec(memory_space=pltpu.VMEM)] * 4,
        out_specs=[pl.BlockSpec(memory_space=pltpu.VMEM)] * 6,
        out_shape=[jax.ShapeDtypeStruct((1, each), jnp.float32)] * 6,
        cost_estimate=BRIEF,
        name="small",
    )(place, *values)
    results = [r.reshape(each) for r in results]
    return results[:3], results[3:]


def per_device(sizes, inputs, flags, w_one, *rest):
    gamma_one, beta_one, decay_one, w_two, gamma_two, beta_two, decay_two, cotangent = rest
    wide, narrow = sizes["wide"], sizes["narrow"]
    n = lax.axis_index("narrow")
    w = lax.axis_index("wide")
    frames = inputs.shape[0] // narrow
    part = inputs.shape[1]
    tiles = part // LANES
    total_frames = inputs.shape[0] * wide
    rows = frames // ROW_LEN
    first = w * inputs.shape[0] + n * frames
    keep = lax.dynamic_slice_in_dim(flags, first, frames, 0).reshape(rows, ROW_LEN)
    keep = (1 - keep).astype(jnp.float32)
    tie = lax.optimization_barrier

    def along(value, merge):
        return merge_all(value, merge, "narrow", narrow)

    def across(value, merge, open_end=False):
        return merge_all(value, merge, "wide", wide, open_end)

    own = jnp.stack([gamma_one, beta_one, decay_one, gamma_two, beta_two, decay_two])
    each = own.shape[1]
    spread = jnp.zeros((6, each * wide * narrow), jnp.float32)
    spread = lax.dynamic_update_slice_in_dim(spread, own, (n * wide + w) * each, 1)

    units = [(j, r) for j in range(tiles) for r in range(rows)]
    quarter = len(units) // 4
    groups_in = [
        ("line", units[:quarter]),
        ("line", units[quarter : 3 * quarter]),
        ("line", units[3 * quarter :]),
    ]
    eighth = len(units) // 8
    groups_out = [
        ("line", units[:eighth]),
        ("line", units[eighth : 5 * eighth]),
        ("line", units[5 * eighth : 6 * eighth]),
        ("line", units[6 * eighth :]),
    ]

    sliced = cotangent.reshape(narrow, rows, ROW_LEN, tiles, LANES)
    held = [jnp.stack([sliced[:, r, :, j] for j, r in group], 1) for _, group in groups_in]

    line = [n ^ k for k in range(narrow)]
    order = jnp.stack([jnp.asarray(q, jnp.int32) for q in line])
    alone = jnp.zeros((1,), jnp.int32)

    def along_line(blocks):
        pairs = [[(i, i ^ k) for i in range(narrow)] for k in range(narrow)]
        return blocks[:1] + [lax.ppermute(blocks[k], "narrow", pairs[k]) for k in range(1, narrow)]

    split = frames // 4
    def frames_for(lo, hi):
        return [lax.dynamic_slice_in_dim(inputs, q * frames + lo, hi - lo, 0) for q in line]

    early = along_line(frames_for(0, split))
    late = frames_for(split, frames)
    shares = gather_rows([w_one, w_two], wide)
    held = [[lax.dynamic_index_in_dim(h, q, 0, keepdims=False) for q in line] for h in held]
    first = held[0]
    shares, early, late, held, spread, keep, first = tie(
        (shares, early, late, held, spread, keep, first)
    )
    late = along_line(late)
    gains = across(spread, add)
    for k in (1, 2):
        gains = gains + lax.ppermute(gains, "narrow", [(i, i ^ k) for i in range(narrow)])
    share_one, share_two = shares[0], shares[1]
    full_one = lax.all_gather(share_one, "wide", axis=0)
    full_one, first = tie((full_one, first))
    first = along_line(first)
    late, held, share_two, gains = tie((late, held, share_two, gains))
    gains_one, gains_two = gains[:3], gains[3:]
    full_two = lax.all_gather(share_two, "wide", axis=0)
    z_one, moments, source = project([early, late], order, full_one)
    moments, first = tie((moments, first))
    grads = [first]
    merge = merge_moments(frames)
    moments = along(moments, merge)
    moments, held = tie((moments, held))
    group = along_line(held[1])
    halves = across(moments, merge, True)
    plain = [("rows", None)]
    states_one, moments_one, ((h_one,),) = forward(
        z_one, halves, gains_one, keep, alone, plain, total_frames
    )
    h_one = h_one.reshape(frames, -1)
    z_two, moments = project([[h_one]], alone, full_two)
    moments, group = tie((moments, group))
    grads.append(group)
    merge = merge_moments(frames)
    moments = along(moments, merge)
    moments, held = tie((moments, held))
    group = along_line(held[2])
    halves = across(moments, merge, True)
    states_two, moments_two, h_two = forward(
        z_two, halves, gains_two, keep, order, groups_out, total_frames
    )
    grads.append(group)

    second = [along_line(h_two[0])]
    dpre, sums = backward(
        grads, order, groups_in, states_two, z_two, moments_two, gains_two, keep, gains_two[:1]
    )
    sums, second[0] = tie((sums, second[0]))
    sums = along(sums, add)
    sums, h_two = tie((sums, h_two))
    group = along_line(h_two[1])
    halves = across(sums, add, True)
    dz_two, level_two, sums_two, (dh_one,) = dproject(
        dpre, z_two, moments_two, gains_two, halves, full_two, alone, total_frames, 0, frames
    )
    center_one, center_two = moments_one[2:3], moments_two[2:3]
    terms_two = weight_terms(h_one, center_two, [dz_two], [level_two])
    terms_two, third = tie((terms_two, h_two[2]))
    third = along_line(third)
    terms_two, dh_one, group = tie((terms_two, dh_one, group))
    second.append(group)
    plane_two = lax.psum_scatter(terms_two, "wide", scatter_dimension=0, tiled=True)
    dh_one = dh_one.reshape(rows, ROW_LEN, -1)
    dpre, sums = backward(
        [[dh_one]], alone, plain, states_one, z_one, moments_one, gains_one, keep, level_two
    )
    sums, third = tie((sums, third))
    second.append(third)
    sums = along(sums, add)
    sums, h_two = tie((sums, h_two))
    group = along_line(h_two[3])
    halves = across(sums, add, True)
    back = functools.partial(
        dproject, dpre, z_one, moments_one, gains_one, halves, full_one, order, total_frames
    )
    split = frames // 4
    dz_early, level_early, sums_one, da_early = back(0, split)
    level_two = sums_one[3:]
    da_early, group = tie((da_early, group))
    second.append(group)
    da_early = along_line(da_early)
    dz_late, level_late, _, da_late = back(split, frames)
    terms_one = weight_terms(source, center_one, [dz_early, dz_late], [level_early, level_late])
    levels = (level_early, level_late)
    da_early, da_late, terms_one, plane_two, levels, second = tie(
        (da_early, da_late, terms_one, plane_two, levels, second)
    )
    plane_one = lax.psum_scatter(terms_one, "wide", scatter_dimension=0, tiled=True)
    da_late = along_line(da_late)
    da_late[1], second = tie((da_late[1], second))
    parts = {}
    for (kind, group), came in zip(groups_out, second, strict=True):
        if kind == "line":
            stacked = jnp.stack(came)
            came = [
                jnp.stack(
                    [lax.dynamic_index_in_dim(stacked, n ^ q, 0, keepdims=False) for q in range(narrow)]
                )
            ]
        for u, unit in enumerate(group):
            parts[unit] = came[0][:, u]
    whole_two = jnp.stack(
        [jnp.concatenate([parts[j, r] for j in range(tiles)], -1) for r in range(rows)], 1
    )
    whole_two = whole_two.reshape(inputs.shape).astype(jnp.float32)
    output = (inputs.astype(jnp.float32) + whole_two).astype(jnp.bfloat16)

    output, levels = tie((output, levels))

    span = plane_one.shape[0]

    blocks = plane_two.reshape(span, narrow, part).transpose(1, 0, 2)
    came_two = lax.all_to_all(blocks, "narrow", split_axis=0, concat_axis=0)
    came_two = [came_two[i] for i in range(narrow)]
    level_one = levels[0] + levels[1]
    k = wide // 2
    while k:
        level_one = level_one + lax.ppermute(level_one, "wide", [(i, i ^ k) for i in range(wide)])
        k //= 2
    columns = [lax.dynamic_slice_in_dim(plane_one, q * part, part, 1) for q in line]
    columns, level_one = tie((columns, level_one))
    came_one = along_line(columns)
    k = narrow // 2
    while k:
        level_one = level_one + lax.ppermute(
            level_one, "narrow", [(i, i ^ k) for i in range(narrow)]
        )
        k //= 2

    grad_inputs = jnp.zeros(inputs.shape, jnp.float32)
    for lo, came in ((0, da_early), (split, da_late)):
        for q, block in zip(line, came, strict=True):
            at = q * frames + lo
            own = lax.dynamic_slice_in_dim(cotangent, at, block.shape[0], 0).astype(jnp.float32)
            grad_inputs = lax.dynamic_update_slice_in_dim(
                grad_inputs, own + block.astype(jnp.float32), at, 0
            )
    came_two, came_one = tie((came_two, came_one))
    dw_two = sum(block.astype(jnp.float32) for block in came_two)
    dw_one = sum(block.astype(jnp.float32) for block in came_one)

    def restored(weight, center, level):
        rows_of = lax.dynamic_slice_in_dim(center, w * span, span, 1).reshape(span, 1)
        return weight + rows_of * lax.dynamic_slice_in_dim(level, n * part, part, 1)

    dw_one = restored(dw_one, center_one, level_one)
    dw_two = restored(dw_two, center_two, level_two)

    place = jnp.asarray(n * wide + w, jnp.int32).reshape(1)
    small_one, small_two = small_gradients(
        place, each, total_frames, sums_one, moments_one, sums_two, moments_two
    )
    return output, grad_inputs, dw_one, *small_one, dw_two, *small_two


def solution(mesh):
    neurons = P(("narrow", "wide"))
    frames = P("wide", "narrow")
    weight = P(None, "narrow")
    small = (neurons, neurons, neurons)
    return jax.shard_map(
        functools.partial(per_device, dict(mesh.shape)),
        mesh=mesh,
        in_specs=(frames, P(), weight, *small, weight, *small, frames),
        out_specs=(frames, frames, frames, *small, frames, *small),
        check_vma=False,
    )
```

```python
import functools
import math

import jax
import jax.numpy as jnp
from jax import lax
from jax.experimental import pallas as pl
from jax.experimental.pallas import tpu as pltpu
from jax.sharding import PartitionSpec as P

ROW_LEN = 512
EPSILON = 1e-05
LOG2E = 1.4426950408889634
LN2 = 0.6931471805599453
LANES = 128
SUB = 16
CHUNK = 64
CHUNK_BACK = 128
VMEM_LIMIT = 56 * 2**20
BOTH = ("narrow", "wide")

params_of = functools.partial(pltpu.CompilerParams, vmem_limit_bytes=VMEM_LIMIT)
SMEM = pl.BlockSpec(memory_space=pltpu.SMEM)
BRIEF = pl.CostEstimate(flops=1, bytes_accessed=1, transcendentals=0)


def whole(shape):
    return pl.BlockSpec(shape, lambda *_: (0,) * len(shape))


def merge_all(value, merge, axis, size, open_end=False):
    k = size
    while k > 1:
        if open_end and k == 2:
            return [value, lax.ppermute(value, axis, [(i, i ^ 1) for i in range(size)])]
        if k % 4 == 0 and not (open_end and k == 4):
            k //= 4
            turns = (k, 2 * k, 3 * k)
        else:
            k //= 2
            turns = (k,)
        others = [lax.ppermute(value, axis, [(i, i ^ t) for i in range(size)]) for t in turns]
        value = merge([value, *others])
    return value


def add(values):
    while len(values) > 1:
        values = [a + b for a, b in zip(values[::2], values[1::2], strict=True)]
    return values[0]


def merge_moments(frames):
    count = [frames]

    def merge(values):
        summed = add(values)
        row = lax.broadcasted_iota(jnp.int32, summed.shape, 0)
        part = 1 / len(values)
        mean = summed[0:1] * part
        gaps = [v[0:1] - mean for v in values]
        squares = add([gap * gap for gap in gaps]) * count[0]
        count[0] *= len(values)
        scale = jnp.where((row == 0) | (row == 2), part, 1.0)
        return summed * scale + jnp.where(row == 1, squares, 0.0)

    return merge


def gather_rows(weights, wide):
    rows = weights[0].shape[0] // wide
    first = lax.axis_index("wide") * rows
    shares = [lax.dynamic_slice_in_dim(weight, first, rows, 0) for weight in weights]
    return lax.all_gather(jnp.stack(shares), "narrow", axis=1)


def project_kernel(blocks, cuts, order, *refs):
    pieces = len(cuts) - 1
    x_refs = [refs[i * blocks : (i + 1) * blocks] for i in range(pieces)]
    w_ref, z_ref, moments_ref, *joined_ref = refs[pieces * blocks :]
    frames, cols = z_ref.shape
    depth = x_refs[0][0].shape[1]
    here = pl.program_id(0)
    step = math.gcd(256, *cuts)
    per_block = w_ref.shape[0] // blocks
    weights = [
        w_ref[pl.ds(order[k] * per_block, per_block)].reshape(depth, cols) for k in range(blocks)
    ]
    sums = jnp.zeros((1, cols), jnp.float32)
    for piece in range(pieces):
        for m in range(cuts[piece], cuts[piece + 1], step):
            acc = None
            for x_ref, weight in zip(x_refs[piece], weights, strict=True):
                x = x_ref[m - cuts[piece] : m - cuts[piece] + step, :]
                term = jnp.dot(x, weight, preferred_element_type=jnp.float32)
                acc = term if acc is None else acc + term
            rounded = acc.astype(jnp.bfloat16)
            z_ref[m : m + step, :] = rounded
            sums += jnp.sum(rounded.astype(jnp.float32), 0, keepdims=True)
    mean = sums / frames
    squares = jnp.zeros((1, cols), jnp.float32)
    for m in range(0, frames, step):
        gap = z_ref[m : m + step, :].astype(jnp.float32) - mean
        squares += jnp.sum(gap * gap, 0, keepdims=True)
    at = pl.ds(pl.multiple_of(here * cols, cols), cols)
    moments_ref[0:1, at] = mean
    moments_ref[1:2, at] = squares
    if not joined_ref:
        own = x_refs[0][0][:, at].astype(jnp.float32)
        moments_ref[2:3, at] = jnp.sum(own, 0, keepdims=True) / frames
        return
    for k in range(blocks):

        @pl.when(here == k)
        def _():
            total = jnp.zeros((1, depth), jnp.float32)
            for piece in range(pieces):
                own = x_refs[piece][k][...]
                joined_ref[0][cuts[piece] : cuts[piece + 1], :] = own
                total += jnp.sum(own.astype(jnp.float32), 0, keepdims=True)
            place = pl.ds(pl.multiple_of(order[k] * depth, depth), depth)
            moments_ref[2:3, place] = total / frames


def project(pieces, order, weight):
    blocks = len(pieces[0])
    depth = pieces[0][0].shape[1]
    cuts = [0]
    for piece in pieces:
        cuts.append(cuts[-1] + piece[0].shape[0])
    frames = cuts[-1]
    row_blocks, steps, span, width = weight.shape
    rows, cols = row_blocks * span, steps * width
    out_shape = [
        jax.ShapeDtypeStruct((frames, cols), jnp.bfloat16),
        jax.ShapeDtypeStruct((3, cols), jnp.float32),
    ]
    out_specs = [pl.BlockSpec((frames, width), lambda i, o: (0, i)), whole((3, cols))]
    if blocks > 1:
        out_shape.append(jax.ShapeDtypeStruct((frames, rows), jnp.bfloat16))
        out_specs.append(pl.BlockSpec((frames, depth), lambda i, o: (0, o[i])))
    flat = [block for piece in pieces for block in piece]
    return pl.pallas_call(
        functools.partial(project_kernel, blocks, cuts),
        grid_spec=pltpu.PrefetchScalarGridSpec(
            num_scalar_prefetch=1,
            grid=(steps,),
            in_specs=[whole(block.shape) for block in flat]
            + [pl.BlockSpec((row_blocks, None, span, width), lambda i, o: (0, i, 0, 0))],
            out_specs=out_specs,
        ),
        out_shape=out_shape,
        compiler_params=params_of(),
        cost_estimate=BRIEF,
        name="project",
    )(order, *flat, weight)


def to_steps(row_ref, lanes_ref, tiles):
    for j in range(tiles):
        lanes_ref[j : j + 1, :] = row_ref[:, j * LANES : (j + 1) * LANES]


def forward_kernel(total_frames, groups, order, keep, mine, other, gains, z_ref, s_ref, moments, *refs):
    *h_refs, vec, state, seq, hold = refs
    rows, chunk, width = z_ref.shape
    tiles = width // LANES

    @pl.when(pl.program_id(0) == 0)
    def _():
        gap = mine[0:1, :] - other[0:1, :]
        squares = mine[1:2, :] + other[1:2, :] + gap * gap * (total_frames / 4)
        scale = gains[0:1, :] * lax.rsqrt(squares / total_frames + EPSILON)
        moments[...] = (mine[...] + other[...]) * 0.5
        moments[1:2, :] = squares
        lanes = [moments[0:1, :], scale * LOG2E, gains[1:2, :] * LOG2E, gains[2:3, :] * LOG2E]
        for i, row in enumerate(lanes):
            for j in range(tiles):
                vec[i, j : j + 1, :] = row[:, j * LANES : (j + 1) * LANES]
        state[...] = jnp.zeros_like(state)

    mean, scale, shift, decay = (vec[i] for i in range(4))
    first = pl.program_id(0) * chunk

    def block(c, running):
        running = list(running)
        for r in range(rows):
            values = z_ref[r, pl.ds(pl.multiple_of(c * SUB, SUB), SUB), :].astype(jnp.float32)
            for j in range(tiles):
                for half in range(SUB // 8):
                    seq[c % 2, r, pl.ds(half * 8 * tiles + j, 8, stride=tiles), :] = values[
                        half * 8 : half * 8 + 8, j * LANES : (j + 1) * LANES
                    ]
        for k in range(SUB):
            for r in range(rows):
                value = (seq[c % 2, r, k * tiles : (k + 1) * tiles, :] - mean) * scale + shift
                before = value + (decay * keep[r, first + c * SUB + k]) * running[r]
                fresh = jnp.where(
                    before > 30.0, before * LN2, jnp.log(1.0 + jnp.exp2(before))
                )
                running[r] = fresh
                hold[c % 2, r, k * tiles : (k + 1) * tiles, :] = fresh
                at = pl.ds(pl.multiple_of((c * SUB + k) * tiles, tiles), tiles)
                s_ref[r, at, :] = fresh.astype(jnp.bfloat16)

        def rounded(r, tile):
            halves = [
                hold[c % 2, r, pl.ds(half * 8 * tiles + tile, 8, stride=tiles), :]
                for half in range(SUB // 8)
            ]
            return jnp.concatenate(halves, 0).astype(jnp.bfloat16)

        place = pl.ds(pl.multiple_of(c * SUB, SUB), SUB)
        left = list(h_refs)
        for kind, units in groups:
            if kind == "rows":
                h_ref = left.pop(0)
                for r in range(rows):
                    for j in range(tiles):
                        h_ref[r, place, j * LANES : (j + 1) * LANES] = rounded(r, j)
            elif kind == "blocks":
                h_ref = left.pop(0)
                per_block = tiles // h_ref.shape[0]
                for q in range(h_ref.shape[0]):
                    for u, (j, r) in enumerate(units):
                        h_ref[q, u, place, :] = rounded(r, q * per_block + j)
            else:
                count = order.shape[0]
                for k in range(count):
                    h_ref = left.pop(0)
                    for u, (j, r) in enumerate(units):
                        h_ref[u, place, :] = rounded(r, order[k] * (tiles // count) + j)
        return tuple(running)

    running = tuple(state[r] for r in range(rows))
    for c in range(chunk // SUB):
        running = block(c, running)
    for r in range(rows):
        state[r] = running[r]


def unit_shapes(groups, blocks, rows, width, length):
    shapes = []
    for kind, units in groups:
        if kind == "rows":
            shapes.append((rows, length, width))
        elif kind == "blocks":
            shapes.append((blocks, len(units), length, LANES))
        else:
            shapes += [(len(units), length, LANES)] * blocks
    return shapes


def unit_spec(shape, at, chunk):
    if len(shape) == 3:
        return pl.BlockSpec((shape[0], chunk, shape[2]), lambda i: (0, at(i), 0))
    return pl.BlockSpec((*shape[:2], chunk, LANES), lambda i: (0, 0, at(i), 0))


def forward(z, moments, gains, keep, order, groups, total_frames):
    rows, length = keep.shape
    width = z.shape[1]
    tiles = width // LANES
    shapes = unit_shapes(groups, order.shape[0], rows, width, length)
    states, merged, *results = pl.pallas_call(
        functools.partial(forward_kernel, total_frames, groups),
        grid=(length // CHUNK,),
        in_specs=[
            SMEM,
            SMEM,
            whole((3, width)),
            whole((3, width)),
            whole((3, width)),
            pl.BlockSpec((rows, CHUNK, width), lambda i: (0, i, 0)),
        ],
        out_specs=[
            pl.BlockSpec((rows, CHUNK * tiles, LANES), lambda i: (0, i, 0)),
            whole((3, width)),
        ]
        + [unit_spec(shape, lambda i: i, CHUNK) for shape in shapes],
        out_shape=[
            jax.ShapeDtypeStruct((rows, length * tiles, LANES), jnp.bfloat16),
            jax.ShapeDtypeStruct((3, width), jnp.float32),
        ]
        + [jax.ShapeDtypeStruct(shape, jnp.bfloat16) for shape in shapes],
        scratch_shapes=[
            pltpu.VMEM((4, tiles, LANES), jnp.float32),
            pltpu.VMEM((rows, tiles, LANES), jnp.float32),
            pltpu.VMEM((2, rows, SUB * tiles, LANES), jnp.float32),
            pltpu.VMEM((2, rows, SUB * tiles, LANES), jnp.float32),
        ],
        compiler_params=params_of(),
        cost_estimate=BRIEF,
        name="forward",
    )(order, keep, *moments, gains, z.reshape(rows, length, width))
    grouped = []
    for kind, _ in groups:
        grouped.append([results.pop(0) for _ in range(order.shape[0] if kind == "line" else 1)])
    return states, merged, grouped


def backward_kernel(groups, order, keep, moments, gains, extra, s_ref, before_ref, z_ref, *refs):
    *g_refs, dpre_ref, out_ref, sums_ref, vec, state, seq, grads = refs
    rows, chunk, width = z_ref.shape
    tiles = width // LANES
    step = pl.program_id(0)
    first = (pl.num_programs(0) - 1 - step) * chunk

    @pl.when(step == 0)
    def _():
        for j in range(tiles):
            vec[j : j + 1, :] = gains[2:3, j * LANES : (j + 1) * LANES]
        state[...] = jnp.zeros_like(state)
        sums_ref[...] = jnp.zeros_like(sums_ref)

    decay = vec[...]
    mean = moments[0:1, :]
    blocks = chunk // SUB

    def block(i, running):
        *running, dsum = running
        c = blocks - 1 - i
        base = pl.multiple_of(c * SUB, SUB)
        def spread(r, tile, values):
            for half in range(SUB // 8):
                seq[r, pl.ds(half * 8 * tiles + tile, 8, stride=tiles), :] = values[
                    half * 8 : half * 8 + 8, :
                ]

        left = list(g_refs)
        for kind, units in groups:
            if kind == "rows":
                g_ref = left.pop(0)
                for r in range(rows):
                    values = g_ref[r, pl.ds(base, SUB), :].astype(jnp.float32)
                    for j in range(tiles):
                        spread(r, j, values[:, j * LANES : (j + 1) * LANES])
            elif kind == "blocks":
                g_ref = left.pop(0)
                per_block = tiles // g_ref.shape[0]
                for q in range(g_ref.shape[0]):
                    for u, (j, r) in enumerate(units):
                        values = g_ref[q, u, pl.ds(base, SUB), :].astype(jnp.float32)
                        spread(r, q * per_block + j, values)
            else:
                count = order.shape[0]
                for k in range(count):
                    g_ref = left.pop(0)
                    for u, (j, r) in enumerate(units):
                        values = g_ref[u, pl.ds(base, SUB), :].astype(jnp.float32)
                        spread(r, order[k] * (tiles // count) + j, values)
        def held_state(r, at):
            rows_at = pl.ds(pl.multiple_of(at * tiles, tiles), tiles)
            return s_ref[r, rows_at, :].astype(jnp.float32)

        states = [held_state(r, c * SUB + SUB - 1) for r in range(rows)]
        for k in range(SUB - 1, -1, -1):
            for r in range(rows):
                at = c * SUB + k
                s = states[r]
                if k > 0:
                    prior = held_state(r, at - 1)
                else:
                    inner = held_state(r, jnp.maximum(at - 1, 0))
                    prior = jnp.where(c > 0, inner, before_ref[r].astype(jnp.float32))
                states[r] = prior
                mark = keep[r, first + at]
                slope = 1.0 - jnp.exp2(s * -LOG2E)
                dpre = (seq[r, k * tiles : (k + 1) * tiles, :] + running[r]) * slope
                held = dpre * mark
                running[r] = held * decay
                dsum = dsum + held * prior
                grads[r, k * tiles : (k + 1) * tiles, :] = dpre
        gb = jnp.zeros((8, width), jnp.float32)
        gg = jnp.zeros((8, width), jnp.float32)
        for r in range(rows):
            gaps = z_ref[r, pl.ds(base, SUB), :].astype(jnp.float32) - mean
            for half in range(SUB // 8):
                dpre = jnp.concatenate(
                    [
                        grads[r, pl.ds(half * 8 * tiles + j, 8, stride=tiles), :]
                        for j in range(tiles)
                    ],
                    1,
                )
                dpre_ref[r, pl.ds(pl.multiple_of(base + half * 8, 8), 8), :] = dpre
                gb += dpre
                gg += dpre * gaps[half * 8 : half * 8 + 8, :]
        sums_ref[0:8, :] += gb
        sums_ref[8:16, :] += gg
        return (*running, dsum)

    start = tuple(state[r] for r in range(rows)) + (state[rows],)
    *running, dsum = lax.fori_loop(0, blocks, block, start)
    for r in range(rows):
        state[r] = running[r]
    state[rows] = dsum

    @pl.when(step == pl.num_programs(0) - 1)
    def _():
        gb = jnp.sum(sums_ref[0:8, :], 0, keepdims=True)
        gg = jnp.sum(sums_ref[8:16, :], 0, keepdims=True)
        out_ref[0:1, :] = gb
        out_ref[1:2, :] = gg
        for j in range(tiles):
            out_ref[2:3, j * LANES : (j + 1) * LANES] = state[rows, j : j + 1, :]
        out_ref[3:4, :] = extra[0:1, :]


def backward(grads, order, groups, states, z, moments, gains, keep, extra):
    rows, length = keep.shape
    width = z.shape[1]
    tiles = width // LANES
    last = length // CHUNK_BACK - 1
    grads = [g for group in grads for g in group]
    dpre, sums = pl.pallas_call(
        functools.partial(backward_kernel, groups),
        grid=(length // CHUNK_BACK,),
        in_specs=[
            SMEM,
            SMEM,
            whole((3, width)),
            whole((3, width)),
            whole(extra.shape),
            pl.BlockSpec((rows, CHUNK_BACK * tiles, LANES), lambda i: (0, last - i, 0)),
            pl.BlockSpec(
                (rows, tiles, LANES), lambda i: (0, jnp.maximum((last - i) * CHUNK_BACK - 1, 0), 0)
            ),
            pl.BlockSpec((rows, CHUNK_BACK, width), lambda i: (0, last - i, 0)),
        ]
        + [unit_spec(g.shape, lambda i: last - i, CHUNK_BACK) for g in grads],
        out_specs=[
            pl.BlockSpec((rows, CHUNK_BACK, width), lambda i: (0, last - i, 0)),
            whole((4, width)),
        ],
        out_shape=[
            jax.ShapeDtypeStruct((rows, length, width), jnp.float32),
            jax.ShapeDtypeStruct((4, width), jnp.float32),
        ],
        scratch_shapes=[
            pltpu.VMEM((16, width), jnp.float32),
            pltpu.VMEM((tiles, LANES), jnp.float32),
            pltpu.VMEM((rows + 1, tiles, LANES), jnp.float32),
            pltpu.VMEM((rows, SUB * tiles, LANES), jnp.float32),
            pltpu.VMEM((rows, SUB * tiles, LANES), jnp.float32),
        ],
        compiler_params=params_of(),
        cost_estimate=BRIEF,
        name="backward",
    )(
        order,
        keep,
        moments,
        gains,
        extra,
        states,
        states,
        z.reshape(rows, length, width),
        *grads,
    )
    return dpre.reshape(rows * length, width), sums


def dproject_kernel(total_frames, order, moments, gains, mine, other, dpre_ref, z_ref, w_ref, *refs):
    dz_ref, level_ref, sums_ref, *da_refs, dz_held, weight, arrived = refs
    here = pl.program_id(0)
    last = pl.num_programs(0) - 1
    width = dpre_ref.shape[1]
    slot = lax.rem(here, 2)

    def fetch(j):
        cols = w_ref.shape[3]
        return pltpu.make_async_copy(
            w_ref.at[:, j], weight.at[:, :, pl.ds(j * cols, cols)], arrived.at[j]
        )

    def differentiate():
        rstd = lax.rsqrt(moments[1:2, :] / total_frames + EPSILON)
        scale = gains[0:1, :] * rstd
        level = (mine[0:1, :] + other[0:1, :]) / total_frames
        slope = (mine[1:2, :] + other[1:2, :]) * (rstd * rstd) / total_frames
        gap = z_ref[...].astype(jnp.float32) - moments[0:1, :]
        dz = (scale * (dpre_ref[...] - level - gap * slope)).astype(jnp.bfloat16)
        dz_ref[...] = dz
        dz_held[slot] = dz
        level_ref[...] += jnp.sum(dz.astype(jnp.float32), 0, keepdims=True)

    def multiply():
        per_part = weight.shape[0] // len(da_refs)
        for k, da_ref in enumerate(da_refs):
            part = weight[pl.ds(order[k] * per_part, per_part)].reshape(-1, width)
            da_ref[...] = lax.dot_general(
                dz_held[1 - slot],
                part,
                (((1,), (1,)), ((), ())),
                preferred_element_type=jnp.float32,
            ).astype(jnp.bfloat16)

    @pl.when(here == 0)
    def _():
        for j in range(w_ref.shape[1]):
            fetch(j).start()
        level_ref[...] = jnp.zeros_like(level_ref)
        sums_ref[...] = mine[...] + other[...]
        differentiate()
        for j in range(w_ref.shape[1]):
            fetch(j).wait()

    @pl.when((here > 0) & (here < last))
    def _():
        multiply()
        differentiate()

    @pl.when(here == last)
    def _():
        multiply()


def dproject(dpre, z, moments, gains, sums, weight, order, total_frames, lo, hi):
    frames, width = hi - lo, z.shape[1]
    row_blocks, col_blocks, span, cols = weight.shape
    parts = order.shape[0]
    depth = row_blocks * span // parts
    step = math.gcd(frames, 256)
    steps = frames // step
    dz, level, merged, *da = pl.pallas_call(
        functools.partial(dproject_kernel, total_frames),
        grid=(steps + 1,),
        in_specs=[
            SMEM,
            whole((3, width)),
            whole((3, width)),
            whole((4, width)),
            whole((4, width)),
            pl.BlockSpec((step, width), lambda i: (jnp.minimum(i, steps - 1) + lo // step, 0)),
            pl.BlockSpec((step, width), lambda i: (jnp.minimum(i, steps - 1) + lo // step, 0)),
            pl.BlockSpec(memory_space=pl.ANY),
        ],
        out_specs=[
            pl.BlockSpec((step, width), lambda i: (jnp.minimum(i, steps - 1), 0)),
            whole((1, width)),
            whole((4, width)),
        ]
        + [pl.BlockSpec((step, depth), lambda i: (jnp.maximum(i - 1, 0), 0))] * parts,
        out_shape=[
            jax.ShapeDtypeStruct((frames, width), jnp.bfloat16),
            jax.ShapeDtypeStruct((1, width), jnp.float32),
            jax.ShapeDtypeStruct((4, width), jnp.float32),
        ]
        + [jax.ShapeDtypeStruct((frames, depth), jnp.bfloat16)] * parts,
        scratch_shapes=[
            pltpu.VMEM((2, step, width), jnp.bfloat16),
            pltpu.VMEM((row_blocks, span, width), jnp.bfloat16),
            pltpu.SemaphoreType.DMA((col_blocks,)),
        ],
        compiler_params=params_of(),
        cost_estimate=BRIEF,
        name="dproject",
    )(order, moments, gains, *sums, dpre, z, weight)
    return dz, level, merged, da


def weight_kernel(pieces, *refs):
    level_refs, dz_refs = refs[:pieces], refs[pieces : 2 * pieces]
    center_ref, source_ref, out_ref = refs[2 * pieces :]
    level = sum(level_ref[...] for level_ref in level_refs)
    center = jnp.transpose(jnp.broadcast_to(center_ref[2:3, :], (8, center_ref.shape[1])))[:, :1]
    terms = -center * level
    lo = 0
    for dz_ref in dz_refs:
        count = dz_ref.shape[0]
        terms += lax.dot_general(
            source_ref[lo : lo + count, :],
            dz_ref[...],
            (((0,), (0,)), ((), ())),
            preferred_element_type=jnp.float32,
        )
        lo += count
    out_ref[...] = terms.astype(jnp.bfloat16)


def weight_terms(source, moments, dz, levels):
    frames, rows = source.shape
    cols = dz[0].shape[1]
    tile = 512
    return pl.pallas_call(
        functools.partial(weight_kernel, len(dz)),
        grid=(rows // tile,),
        in_specs=[whole((1, cols))] * len(dz)
        + [whole(d.shape) for d in dz]
        + [
            pl.BlockSpec((3, tile), lambda i: (0, i)),
            pl.BlockSpec((frames, tile), lambda i: (0, i)),
        ],
        out_specs=pl.BlockSpec((tile, cols), lambda i: (i, 0)),
        out_shape=jax.ShapeDtypeStruct((rows, cols), jnp.bfloat16),
        compiler_params=params_of(),
        cost_estimate=BRIEF,
        name="weight",
    )(*levels, *dz, moments, source)


def small_kernel(total_frames, place, *refs):
    ins, outs = refs[:4], refs[4:]
    each = outs[0].shape[1]
    first = place[0] * each
    aligned = pl.multiple_of(first // LANES * LANES, LANES)
    turn = lax.rem(LANES - (first - aligned), LANES)

    def own(ref, row):
        return pltpu.roll(ref[row : row + 1, pl.ds(aligned, LANES)], turn, 1)[:, :each]

    for i in range(2):
        sums, moments = ins[2 * i : 2 * i + 2]
        rstd = lax.rsqrt(own(moments, 1) / total_frames + EPSILON)
        outs[3 * i][...] = own(sums, 1) * rstd
        outs[3 * i + 1][...] = own(sums, 0)
        outs[3 * i + 2][...] = own(sums, 2)


def small_gradients(place, each, total_frames, *values):
    results = pl.pallas_call(
        functools.partial(small_kernel, total_frames),
        in_specs=[SMEM] + [pl.BlockSpec(memory_space=pltpu.VMEM)] * 4,
        out_specs=[pl.BlockSpec(memory_space=pltpu.VMEM)] * 6,
        out_shape=[jax.ShapeDtypeStruct((1, each), jnp.float32)] * 6,
        cost_estimate=BRIEF,
        name="small",
    )(place, *values)
    results = [r.reshape(each) for r in results]
    return results[:3], results[3:]


def per_device(sizes, inputs, flags, w_one, *rest):
    gamma_one, beta_one, decay_one, w_two, gamma_two, beta_two, decay_two, cotangent = rest
    wide, narrow = sizes["wide"], sizes["narrow"]
    n = lax.axis_index("narrow")
    w = lax.axis_index("wide")
    frames = inputs.shape[0] // narrow
    part = inputs.shape[1]
    tiles = part // LANES
    total_frames = inputs.shape[0] * wide
    rows = frames // ROW_LEN
    first = w * inputs.shape[0] + n * frames
    keep = lax.dynamic_slice_in_dim(flags, first, frames, 0).reshape(rows, ROW_LEN)
    keep = (1 - keep).astype(jnp.float32)
    tie = lax.optimization_barrier

    def along(value, merge):
        return merge_all(value, merge, "narrow", narrow)

    def across(value, merge, open_end=False):
        return merge_all(value, merge, "wide", wide, open_end)

    own = jnp.stack([gamma_one, beta_one, decay_one, gamma_two, beta_two, decay_two])
    each = own.shape[1]
    spread = jnp.zeros((6, each * wide * narrow), jnp.float32)
    spread = lax.dynamic_update_slice_in_dim(spread, own, (n * wide + w) * each, 1)

    units = [(j, r) for j in range(tiles) for r in range(rows)]
    quarter = len(units) // 4
    groups_in = [
        ("line", units[:quarter]),
        ("line", units[quarter : 3 * quarter]),
        ("line", units[3 * quarter :]),
    ]
    eighth = len(units) // 8
    groups_out = [
        ("line", units[:eighth]),
        ("line", units[eighth : 5 * eighth]),
        ("line", units[5 * eighth : 6 * eighth]),
        ("line", units[6 * eighth :]),
    ]

    sliced = cotangent.reshape(narrow, rows, ROW_LEN, tiles, LANES)
    held = [jnp.stack([sliced[:, r, :, j] for j, r in group], 1) for _, group in groups_in]

    line = [n ^ k for k in range(narrow)]
    order = jnp.stack([jnp.asarray(q, jnp.int32) for q in line])
    alone = jnp.zeros((1,), jnp.int32)

    def along_line(blocks):
        pairs = [[(i, i ^ k) for i in range(narrow)] for k in range(narrow)]
        return blocks[:1] + [lax.ppermute(blocks[k], "narrow", pairs[k]) for k in range(1, narrow)]

    split = frames // 4
    def frames_for(lo, hi):
        return [lax.dynamic_slice_in_dim(inputs, q * frames + lo, hi - lo, 0) for q in line]

    early = along_line(frames_for(0, split))
    late = frames_for(split, frames)
    shares = gather_rows([w_one, w_two], wide)
    held = [[lax.dynamic_index_in_dim(h, q, 0, keepdims=False) for q in line] for h in held]
    first = held[0]
    shares, early, late, held, spread, keep, first, order = tie(
        (shares, early, late, held, spread, keep, first, order)
    )
    late = along_line(late)
    gains = across(spread, add)
    for k in (1, 2):
        gains = gains + lax.ppermute(gains, "narrow", [(i, i ^ k) for i in range(narrow)])
    share_one, share_two = shares[0], shares[1]
    full_one = lax.all_gather(share_one, "wide", axis=0)
    full_one, first = tie((full_one, first))
    first = along_line(first)
    late, held, share_two, gains = tie((late, held, share_two, gains))
    gains_one, gains_two = gains[:3], gains[3:]
    full_two = lax.all_gather(share_two, "wide", axis=0)
    z_one, moments, source = project([early, late], order, full_one)
    moments, first = tie((moments, first))
    grads = [first]
    merge = merge_moments(frames)
    moments = along(moments, merge)
    moments, held = tie((moments, held))
    group = along_line(held[1])
    halves = across(moments, merge, True)
    plain = [("rows", None)]
    states_one, moments_one, ((h_one,),) = forward(
        z_one, halves, gains_one, keep, alone, plain, total_frames
    )
    h_one = h_one.reshape(frames, -1)
    z_two, moments = project([[h_one]], alone, full_two)
    moments, group = tie((moments, group))
    grads.append(group)
    merge = merge_moments(frames)
    moments = along(moments, merge)
    moments, held = tie((moments, held))
    group = along_line(held[2])
    halves = across(moments, merge, True)
    states_two, moments_two, h_two = forward(
        z_two, halves, gains_two, keep, order, groups_out, total_frames
    )
    grads.append(group)

    second = [along_line(h_two[0])]
    dpre, sums = backward(
        grads, order, groups_in, states_two, z_two, moments_two, gains_two, keep, gains_two
    )
    sums, second[0] = tie((sums, second[0]))
    sums = along(sums, add)
    sums, h_two = tie((sums, h_two))
    group = along_line(h_two[1])
    halves = across(sums, add, True)
    dz_two, level_two, sums_two, (dh_one,) = dproject(
        dpre, z_two, moments_two, gains_two, halves, full_two, alone, total_frames, 0, frames
    )
    terms_two = weight_terms(h_one, moments_two, [dz_two], [level_two])
    terms_two, third = tie((terms_two, h_two[2]))
    third = along_line(third)
    terms_two, dh_one, group = tie((terms_two, dh_one, group))
    second.append(group)
    plane_two = lax.psum_scatter(terms_two, "wide", scatter_dimension=0, tiled=True)
    dh_one = dh_one.reshape(rows, ROW_LEN, -1)
    dpre, sums = backward(
        [[dh_one]], alone, plain, states_one, z_one, moments_one, gains_one, keep, level_two
    )
    sums, third = tie((sums, third))
    second.append(third)
    sums = along(sums, add)
    sums, h_two = tie((sums, h_two))
    group = along_line(h_two[3])
    halves = across(sums, add, True)
    back = functools.partial(
        dproject, dpre, z_one, moments_one, gains_one, halves, full_one, order, total_frames
    )
    split = frames // 4
    dz_early, level_early, sums_one, da_early = back(0, split)
    da_early, group = tie((da_early, group))
    second.append(group)
    da_early = along_line(da_early)
    dz_late, level_late, _, da_late = back(split, frames)
    terms_one = weight_terms(source, moments_one, [dz_early, dz_late], [level_early, level_late])
    levels = (level_early, level_late)
    da_early, da_late, terms_one, plane_two, levels, second = tie(
        (da_early, da_late, terms_one, plane_two, levels, second)
    )
    plane_one = lax.psum_scatter(terms_one, "wide", scatter_dimension=0, tiled=True)
    da_late = along_line(da_late)
    da_late[1], second, moments_one, moments_two, sums_one, sums_two = tie(
        (da_late[1], second, moments_one, moments_two, sums_one, sums_two)
    )
    parts = {}
    for (kind, group), came in zip(groups_out, second, strict=True):
        if kind == "line":
            stacked = jnp.stack(came)
            came = [
                jnp.stack(
                    [lax.dynamic_index_in_dim(stacked, n ^ q, 0, keepdims=False) for q in range(narrow)]
                )
            ]
        for u, unit in enumerate(group):
            parts[unit] = came[0][:, u]
    whole_two = jnp.stack(
        [jnp.concatenate([parts[j, r] for j in range(tiles)], -1) for r in range(rows)], 1
    )
    whole_two = whole_two.reshape(inputs.shape).astype(jnp.float32)
    output = (inputs.astype(jnp.float32) + whole_two).astype(jnp.bfloat16)

    output, levels = tie((output, levels))

    span = plane_one.shape[0]

    blocks = plane_two.reshape(span, narrow, part).transpose(1, 0, 2)
    came_two = lax.all_to_all(blocks, "narrow", split_axis=0, concat_axis=0)
    came_two = [came_two[i] for i in range(narrow)]
    level_one = levels[0] + levels[1]
    k = wide // 2
    while k:
        level_one = level_one + lax.ppermute(level_one, "wide", [(i, i ^ k) for i in range(wide)])
        k //= 2
    columns = [lax.dynamic_slice_in_dim(plane_one, q * part, part, 1) for q in line]
    columns, level_one = tie((columns, level_one))
    came_one = along_line(columns)
    k = narrow // 2
    while k:
        level_one = level_one + lax.ppermute(
            level_one, "narrow", [(i, i ^ k) for i in range(narrow)]
        )
        k //= 2

    grad_inputs = jnp.zeros(inputs.shape, jnp.float32)
    for lo, came in ((0, da_early), (split, da_late)):
        for q, block in zip(line, came, strict=True):
            at = q * frames + lo
            own = lax.dynamic_slice_in_dim(cotangent, at, block.shape[0], 0).astype(jnp.float32)
            grad_inputs = lax.dynamic_update_slice_in_dim(
                grad_inputs, own + block.astype(jnp.float32), at, 0
            )
    came_two, came_one = tie((came_two, came_one))
    dw_two = sum(block.astype(jnp.float32) for block in came_two)
    dw_one = sum(block.astype(jnp.float32) for block in came_one)

    def restored(weight, moments, level, row):
        rows_of = lax.dynamic_slice(moments, (2, w * span), (1, span)).reshape(span, 1)
        return weight + rows_of * lax.dynamic_slice(level, (row, n * part), (1, part))

    dw_one = restored(dw_one, moments_one, level_one, 0)
    dw_two = restored(dw_two, moments_two, sums_one, 3)

    place = jnp.asarray(n * wide + w, jnp.int32).reshape(1)
    small_one, small_two = small_gradients(
        place, each, total_frames, sums_one, moments_one, sums_two, moments_two
    )
    return output, grad_inputs, dw_one, *small_one, dw_two, *small_two


def solution(mesh):
    neurons = P(("narrow", "wide"))
    frames = P("wide", "narrow")
    weight = P(None, "narrow")
    small = (neurons, neurons, neurons)
    return jax.shard_map(
        functools.partial(per_device, dict(mesh.shape)),
        mesh=mesh,
        in_specs=(frames, P(), weight, *small, weight, *small, frames),
        out_specs=(frames, frames, frames, *small, frames, *small),
        check_vma=False,
    )
```

```python
import functools
import math

import jax
import jax.numpy as jnp
from jax import lax
from jax.experimental import pallas as pl
from jax.experimental.pallas import tpu as pltpu
from jax.sharding import PartitionSpec as P

ROW_LEN = 512
EPSILON = 1e-05
LOG2E = 1.4426950408889634
LN2 = 0.6931471805599453
LANES = 128
SUB = 16
CHUNK = 64
CHUNK_BACK = 128
VMEM_LIMIT = 56 * 2**20
BOTH = ("narrow", "wide")

params_of = functools.partial(pltpu.CompilerParams, vmem_limit_bytes=VMEM_LIMIT)
SMEM = pl.BlockSpec(memory_space=pltpu.SMEM)
BRIEF = pl.CostEstimate(flops=1, bytes_accessed=1, transcendentals=0)


def whole(shape):
    return pl.BlockSpec(shape, lambda *_: (0,) * len(shape))


def merge_all(value, merge, axis, size, open_end=False):
    k = size
    while k > 1:
        if open_end and k == 2:
            return [value, lax.ppermute(value, axis, [(i, i ^ 1) for i in range(size)])]
        if k % 4 == 0 and not (open_end and k == 4):
            k //= 4
            turns = (k, 2 * k, 3 * k)
        else:
            k //= 2
            turns = (k,)
        others = [lax.ppermute(value, axis, [(i, i ^ t) for i in range(size)]) for t in turns]
        value = merge([value, *others])
    return value


def add(values):
    while len(values) > 1:
        values = [a + b for a, b in zip(values[::2], values[1::2], strict=True)]
    return values[0]


def merge_moments(frames):
    count = [frames]

    def merge(values):
        summed = add(values)
        row = lax.broadcasted_iota(jnp.int32, summed.shape, 0)
        part = 1 / len(values)
        mean = summed[0:1] * part
        gaps = [v[0:1] - mean for v in values]
        squares = add([gap * gap for gap in gaps]) * count[0]
        count[0] *= len(values)
        scale = jnp.where((row == 0) | (row == 2), part, 1.0)
        return summed * scale + jnp.where(row == 1, squares, 0.0)

    return merge


def gather_rows(weights, wide):
    rows = weights[0].shape[0] // wide
    first = lax.axis_index("wide") * rows
    shares = [lax.dynamic_slice_in_dim(weight, first, rows, 0) for weight in weights]
    return lax.all_gather(jnp.stack(shares), "narrow", axis=1)


def project_kernel(blocks, cuts, order, *refs):
    pieces = len(cuts) - 1
    x_refs = [refs[i * blocks : (i + 1) * blocks] for i in range(pieces)]
    w_ref, z_ref, moments_ref, *joined_ref = refs[pieces * blocks :]
    frames, cols = z_ref.shape
    depth = x_refs[0][0].shape[1]
    here = pl.program_id(0)
    step = math.gcd(256, *cuts)
    per_block = w_ref.shape[0] // blocks
    weights = [
        w_ref[pl.ds(order[k] * per_block, per_block)].reshape(depth, cols) for k in range(blocks)
    ]
    sums = jnp.zeros((1, cols), jnp.float32)
    for piece in range(pieces):
        for m in range(cuts[piece], cuts[piece + 1], step):
            acc = None
            for x_ref, weight in zip(x_refs[piece], weights, strict=True):
                x = x_ref[m - cuts[piece] : m - cuts[piece] + step, :]
                term = jnp.dot(x, weight, preferred_element_type=jnp.float32)
                acc = term if acc is None else acc + term
            rounded = acc.astype(jnp.bfloat16)
            z_ref[m : m + step, :] = rounded
            sums += jnp.sum(rounded.astype(jnp.float32), 0, keepdims=True)
    mean = sums / frames
    squares = jnp.zeros((1, cols), jnp.float32)
    for m in range(0, frames, step):
        gap = z_ref[m : m + step, :].astype(jnp.float32) - mean
        squares += jnp.sum(gap * gap, 0, keepdims=True)
    at = pl.ds(pl.multiple_of(here * cols, cols), cols)
    moments_ref[0:1, at] = mean
    moments_ref[1:2, at] = squares
    if not joined_ref:
        own = x_refs[0][0][:, at].astype(jnp.float32)
        moments_ref[2:3, at] = jnp.sum(own, 0, keepdims=True) / frames
        return
    for k in range(blocks):

        @pl.when(here == k)
        def _():
            total = jnp.zeros((1, depth), jnp.float32)
            for piece in range(pieces):
                own = x_refs[piece][k][...]
                joined_ref[0][cuts[piece] : cuts[piece + 1], :] = own
                total += jnp.sum(own.astype(jnp.float32), 0, keepdims=True)
            place = pl.ds(pl.multiple_of(order[k] * depth, depth), depth)
            moments_ref[2:3, place] = total / frames


def project(pieces, order, weight):
    blocks = len(pieces[0])
    depth = pieces[0][0].shape[1]
    cuts = [0]
    for piece in pieces:
        cuts.append(cuts[-1] + piece[0].shape[0])
    frames = cuts[-1]
    row_blocks, steps, span, width = weight.shape
    rows, cols = row_blocks * span, steps * width
    out_shape = [
        jax.ShapeDtypeStruct((frames, cols), jnp.bfloat16),
        jax.ShapeDtypeStruct((3, cols), jnp.float32),
    ]
    out_specs = [pl.BlockSpec((frames, width), lambda i, o: (0, i)), whole((3, cols))]
    if blocks > 1:
        out_shape.append(jax.ShapeDtypeStruct((frames, rows), jnp.bfloat16))
        out_specs.append(pl.BlockSpec((frames, depth), lambda i, o: (0, o[i])))
    flat = [block for piece in pieces for block in piece]
    return pl.pallas_call(
        functools.partial(project_kernel, blocks, cuts),
        grid_spec=pltpu.PrefetchScalarGridSpec(
            num_scalar_prefetch=1,
            grid=(steps,),
            in_specs=[whole(block.shape) for block in flat]
            + [pl.BlockSpec((row_blocks, None, span, width), lambda i, o: (0, i, 0, 0))],
            out_specs=out_specs,
        ),
        out_shape=out_shape,
        compiler_params=params_of(),
        cost_estimate=BRIEF,
        name="project",
    )(order, *flat, weight)


def to_steps(row_ref, lanes_ref, tiles):
    for j in range(tiles):
        lanes_ref[j : j + 1, :] = row_ref[:, j * LANES : (j + 1) * LANES]


def forward_kernel(total_frames, groups, order, keep, mine, other, gains, z_ref, s_ref, moments, *refs):
    *h_refs, vec, state, seq, hold = refs
    rows, chunk, width = z_ref.shape
    tiles = width // LANES

    @pl.when(pl.program_id(0) == 0)
    def _():
        gap = mine[0:1, :] - other[0:1, :]
        squares = mine[1:2, :] + other[1:2, :] + gap * gap * (total_frames / 4)
        scale = gains[0:1, :] * lax.rsqrt(squares / total_frames + EPSILON)
        moments[...] = (mine[...] + other[...]) * 0.5
        moments[1:2, :] = squares
        lanes = [moments[0:1, :], scale * LOG2E, gains[1:2, :] * LOG2E, gains[2:3, :] * LOG2E]
        for i, row in enumerate(lanes):
            for j in range(tiles):
                vec[i, j : j + 1, :] = row[:, j * LANES : (j + 1) * LANES]
        state[...] = jnp.zeros_like(state)

    mean, scale, shift, decay = (vec[i] for i in range(4))
    first = pl.program_id(0) * chunk

    def block(c, running):
        running = list(running)
        for r in range(rows):
            values = z_ref[r, pl.ds(pl.multiple_of(c * SUB, SUB), SUB), :].astype(jnp.float32)
            for j in range(tiles):
                for half in range(SUB // 8):
                    seq[c % 2, r, pl.ds(half * 8 * tiles + j, 8, stride=tiles), :] = values[
                        half * 8 : half * 8 + 8, j * LANES : (j + 1) * LANES
                    ]
        for k in range(SUB):
            for r in range(rows):
                value = (seq[c % 2, r, k * tiles : (k + 1) * tiles, :] - mean) * scale + shift
                before = value + (decay * keep[r, first + c * SUB + k]) * running[r]
                fresh = jnp.where(
                    before > 30.0, before * LN2, jnp.log(1.0 + jnp.exp2(before))
                )
                running[r] = fresh
                hold[c % 2, r, k * tiles : (k + 1) * tiles, :] = fresh
                at = pl.ds(pl.multiple_of((c * SUB + k) * tiles, tiles), tiles)
                s_ref[r, at, :] = fresh.astype(jnp.bfloat16)

        def rounded(r, tile):
            halves = [
                hold[c % 2, r, pl.ds(half * 8 * tiles + tile, 8, stride=tiles), :]
                for half in range(SUB // 8)
            ]
            return jnp.concatenate(halves, 0).astype(jnp.bfloat16)

        place = pl.ds(pl.multiple_of(c * SUB, SUB), SUB)
        left = list(h_refs)
        for kind, units in groups:
            if kind == "rows":
                h_ref = left.pop(0)
                for r in range(rows):
                    for j in range(tiles):
                        h_ref[r, place, j * LANES : (j + 1) * LANES] = rounded(r, j)
            elif kind == "blocks":
                h_ref = left.pop(0)
                per_block = tiles // h_ref.shape[0]
                for q in range(h_ref.shape[0]):
                    for u, (j, r) in enumerate(units):
                        h_ref[q, u, place, :] = rounded(r, q * per_block + j)
            else:
                count = order.shape[0]
                for k in range(count):
                    h_ref = left.pop(0)
                    for u, (j, r) in enumerate(units):
                        h_ref[u, place, :] = rounded(r, order[k] * (tiles // count) + j)
        return tuple(running)

    running = tuple(state[r] for r in range(rows))
    for c in range(chunk // SUB):
        running = block(c, running)
    for r in range(rows):
        state[r] = running[r]


def unit_shapes(groups, blocks, rows, width, length):
    shapes = []
    for kind, units in groups:
        if kind == "rows":
            shapes.append((rows, length, width))
        elif kind == "blocks":
            shapes.append((blocks, len(units), length, LANES))
        else:
            shapes += [(len(units), length, LANES)] * blocks
    return shapes


def unit_spec(shape, at, chunk):
    if len(shape) == 3:
        return pl.BlockSpec((shape[0], chunk, shape[2]), lambda i: (0, at(i), 0))
    return pl.BlockSpec((*shape[:2], chunk, LANES), lambda i: (0, 0, at(i), 0))


def forward(z, moments, gains, keep, order, groups, total_frames):
    rows, length = keep.shape
    width = z.shape[1]
    tiles = width // LANES
    shapes = unit_shapes(groups, order.shape[0], rows, width, length)
    states, merged, *results = pl.pallas_call(
        functools.partial(forward_kernel, total_frames, groups),
        grid=(length // CHUNK,),
        in_specs=[
            SMEM,
            SMEM,
            whole((3, width)),
            whole((3, width)),
            whole((3, width)),
            pl.BlockSpec((rows, CHUNK, width), lambda i: (0, i, 0)),
        ],
        out_specs=[
            pl.BlockSpec((rows, CHUNK * tiles, LANES), lambda i: (0, i, 0)),
            whole((3, width)),
        ]
        + [unit_spec(shape, lambda i: i, CHUNK) for shape in shapes],
        out_shape=[
            jax.ShapeDtypeStruct((rows, length * tiles, LANES), jnp.bfloat16),
            jax.ShapeDtypeStruct((3, width), jnp.float32),
        ]
        + [jax.ShapeDtypeStruct(shape, jnp.bfloat16) for shape in shapes],
        scratch_shapes=[
            pltpu.VMEM((4, tiles, LANES), jnp.float32),
            pltpu.VMEM((rows, tiles, LANES), jnp.float32),
            pltpu.VMEM((2, rows, SUB * tiles, LANES), jnp.float32),
            pltpu.VMEM((2, rows, SUB * tiles, LANES), jnp.float32),
        ],
        compiler_params=params_of(),
        cost_estimate=BRIEF,
        name="forward",
    )(order, keep, *moments, gains, z.reshape(rows, length, width))
    grouped = []
    for kind, _ in groups:
        grouped.append([results.pop(0) for _ in range(order.shape[0] if kind == "line" else 1)])
    return states, merged, grouped


def backward_kernel(groups, order, keep, moments, gains, extra, s_ref, before_ref, z_ref, *refs):
    *g_refs, dpre_ref, out_ref, sums_ref, vec, state, seq, grads = refs
    rows, chunk, width = z_ref.shape
    tiles = width // LANES
    step = pl.program_id(0)
    first = (pl.num_programs(0) - 1 - step) * chunk

    @pl.when(step == 0)
    def _():
        for j in range(tiles):
            vec[j : j + 1, :] = gains[2:3, j * LANES : (j + 1) * LANES]
        state[...] = jnp.zeros_like(state)
        sums_ref[...] = jnp.zeros_like(sums_ref)

    decay = vec[...]
    mean = moments[0:1, :]
    blocks = chunk // SUB

    def block(i, running):
        *running, dsum = running
        c = blocks - 1 - i
        base = pl.multiple_of(c * SUB, SUB)
        def spread(r, tile, values):
            for half in range(SUB // 8):
                seq[r, pl.ds(half * 8 * tiles + tile, 8, stride=tiles), :] = values[
                    half * 8 : half * 8 + 8, :
                ]

        left = list(g_refs)
        for kind, units in groups:
            if kind == "rows":
                g_ref = left.pop(0)
                for r in range(rows):
                    values = g_ref[r, pl.ds(base, SUB), :].astype(jnp.float32)
                    for j in range(tiles):
                        spread(r, j, values[:, j * LANES : (j + 1) * LANES])
            elif kind == "blocks":
                g_ref = left.pop(0)
                per_block = tiles // g_ref.shape[0]
                for q in range(g_ref.shape[0]):
                    for u, (j, r) in enumerate(units):
                        values = g_ref[q, u, pl.ds(base, SUB), :].astype(jnp.float32)
                        spread(r, q * per_block + j, values)
            else:
                count = order.shape[0]
                for k in range(count):
                    g_ref = left.pop(0)
                    for u, (j, r) in enumerate(units):
                        values = g_ref[u, pl.ds(base, SUB), :].astype(jnp.float32)
                        spread(r, order[k] * (tiles // count) + j, values)
        def held_state(r, at):
            rows_at = pl.ds(pl.multiple_of(at * tiles, tiles), tiles)
            return s_ref[r, rows_at, :].astype(jnp.float32)

        states = [held_state(r, c * SUB + SUB - 1) for r in range(rows)]
        for k in range(SUB - 1, -1, -1):
            for r in range(rows):
                at = c * SUB + k
                s = states[r]
                if k > 0:
                    prior = held_state(r, at - 1)
                else:
                    inner = held_state(r, jnp.maximum(at - 1, 0))
                    prior = jnp.where(c > 0, inner, before_ref[r].astype(jnp.float32))
                states[r] = prior
                mark = keep[r, first + at]
                slope = 1.0 - jnp.exp2(s * -LOG2E)
                dpre = (seq[r, k * tiles : (k + 1) * tiles, :] + running[r]) * slope
                held = dpre * mark
                running[r] = held * decay
                dsum = dsum + held * prior
                grads[r, k * tiles : (k + 1) * tiles, :] = dpre
        gb = jnp.zeros((8, width), jnp.float32)
        gg = jnp.zeros((8, width), jnp.float32)
        for r in range(rows):
            gaps = z_ref[r, pl.ds(base, SUB), :].astype(jnp.float32) - mean
            for half in range(SUB // 8):
                dpre = jnp.concatenate(
                    [
                        grads[r, pl.ds(half * 8 * tiles + j, 8, stride=tiles), :]
                        for j in range(tiles)
                    ],
                    1,
                )
                dpre_ref[r, pl.ds(pl.multiple_of(base + half * 8, 8), 8), :] = dpre
                gb += dpre
                gg += dpre * gaps[half * 8 : half * 8 + 8, :]
        sums_ref[0:8, :] += gb
        sums_ref[8:16, :] += gg
        return (*running, dsum)

    start = tuple(state[r] for r in range(rows)) + (state[rows],)
    *running, dsum = lax.fori_loop(0, blocks, block, start)
    for r in range(rows):
        state[r] = running[r]
    state[rows] = dsum

    @pl.when(step == pl.num_programs(0) - 1)
    def _():
        gb = jnp.sum(sums_ref[0:8, :], 0, keepdims=True)
        gg = jnp.sum(sums_ref[8:16, :], 0, keepdims=True)
        out_ref[0:1, :] = gb
        out_ref[1:2, :] = gg
        for j in range(tiles):
            out_ref[2:3, j * LANES : (j + 1) * LANES] = state[rows, j : j + 1, :]
        out_ref[3:4, :] = extra[0:1, :]


def backward(grads, order, groups, states, z, moments, gains, keep, extra):
    rows, length = keep.shape
    width = z.shape[1]
    tiles = width // LANES
    last = length // CHUNK_BACK - 1
    grads = [g for group in grads for g in group]
    dpre, sums = pl.pallas_call(
        functools.partial(backward_kernel, groups),
        grid=(length // CHUNK_BACK,),
        in_specs=[
            SMEM,
            SMEM,
            whole((3, width)),
            whole((3, width)),
            whole(extra.shape),
            pl.BlockSpec((rows, CHUNK_BACK * tiles, LANES), lambda i: (0, last - i, 0)),
            pl.BlockSpec(
                (rows, tiles, LANES), lambda i: (0, jnp.maximum((last - i) * CHUNK_BACK - 1, 0), 0)
            ),
            pl.BlockSpec((rows, CHUNK_BACK, width), lambda i: (0, last - i, 0)),
        ]
        + [unit_spec(g.shape, lambda i: last - i, CHUNK_BACK) for g in grads],
        out_specs=[
            pl.BlockSpec((rows, CHUNK_BACK, width), lambda i: (0, last - i, 0)),
            whole((4, width)),
        ],
        out_shape=[
            jax.ShapeDtypeStruct((rows, length, width), jnp.float32),
            jax.ShapeDtypeStruct((4, width), jnp.float32),
        ],
        scratch_shapes=[
            pltpu.VMEM((16, width), jnp.float32),
            pltpu.VMEM((tiles, LANES), jnp.float32),
            pltpu.VMEM((rows + 1, tiles, LANES), jnp.float32),
            pltpu.VMEM((rows, SUB * tiles, LANES), jnp.float32),
            pltpu.VMEM((rows, SUB * tiles, LANES), jnp.float32),
        ],
        compiler_params=params_of(),
        cost_estimate=BRIEF,
        name="backward",
    )(
        order,
        keep,
        moments,
        gains,
        extra,
        states,
        states,
        z.reshape(rows, length, width),
        *grads,
    )
    return dpre.reshape(rows * length, width), sums


def dproject_kernel(total_frames, order, moments, gains, mine, other, dpre_ref, z_ref, w_ref, *refs):
    dz_ref, level_ref, sums_ref, *da_refs, dz_held, weight, arrived = refs
    here = pl.program_id(0)
    last = pl.num_programs(0) - 1
    width = dpre_ref.shape[1]
    slot = lax.rem(here, 2)

    def fetch(j):
        cols = w_ref.shape[3]
        return pltpu.make_async_copy(
            w_ref.at[:, j], weight.at[:, :, pl.ds(j * cols, cols)], arrived.at[j]
        )

    def differentiate():
        rstd = lax.rsqrt(moments[1:2, :] / total_frames + EPSILON)
        scale = gains[0:1, :] * rstd
        level = (mine[0:1, :] + other[0:1, :]) / total_frames
        slope = (mine[1:2, :] + other[1:2, :]) * (rstd * rstd) / total_frames
        gap = z_ref[...].astype(jnp.float32) - moments[0:1, :]
        dz = (scale * (dpre_ref[...] - level - gap * slope)).astype(jnp.bfloat16)
        dz_ref[...] = dz
        dz_held[slot] = dz
        level_ref[...] += jnp.sum(dz.astype(jnp.float32), 0, keepdims=True)

    def multiply():
        per_part = weight.shape[0] // len(da_refs)
        for k, da_ref in enumerate(da_refs):
            part = weight[pl.ds(order[k] * per_part, per_part)].reshape(-1, width)
            da_ref[...] = lax.dot_general(
                dz_held[1 - slot],
                part,
                (((1,), (1,)), ((), ())),
                preferred_element_type=jnp.float32,
            ).astype(jnp.bfloat16)

    @pl.when(here == 0)
    def _():
        for j in range(w_ref.shape[1]):
            fetch(j).start()
        level_ref[...] = jnp.zeros_like(level_ref)
        sums_ref[...] = mine[...] + other[...]
        differentiate()
        for j in range(w_ref.shape[1]):
            fetch(j).wait()

    @pl.when((here > 0) & (here < last))
    def _():
        multiply()
        differentiate()

    @pl.when(here == last)
    def _():
        multiply()


def dproject(dpre, z, moments, gains, sums, weight, order, total_frames, lo, hi):
    frames, width = hi - lo, z.shape[1]
    row_blocks, col_blocks, span, cols = weight.shape
    parts = order.shape[0]
    depth = row_blocks * span // parts
    step = math.gcd(frames, 256)
    steps = frames // step
    dz, level, merged, *da = pl.pallas_call(
        functools.partial(dproject_kernel, total_frames),
        grid=(steps + 1,),
        in_specs=[
            SMEM,
            whole((3, width)),
            whole((3, width)),
            whole((4, width)),
            whole((4, width)),
            pl.BlockSpec((step, width), lambda i: (jnp.minimum(i, steps - 1) + lo // step, 0)),
            pl.BlockSpec((step, width), lambda i: (jnp.minimum(i, steps - 1) + lo // step, 0)),
            pl.BlockSpec(memory_space=pl.ANY),
        ],
        out_specs=[
            pl.BlockSpec((step, width), lambda i: (jnp.minimum(i, steps - 1), 0)),
            whole((1, width)),
            whole((4, width)),
        ]
        + [pl.BlockSpec((step, depth), lambda i: (jnp.maximum(i - 1, 0), 0))] * parts,
        out_shape=[
            jax.ShapeDtypeStruct((frames, width), jnp.bfloat16),
            jax.ShapeDtypeStruct((1, width), jnp.float32),
            jax.ShapeDtypeStruct((4, width), jnp.float32),
        ]
        + [jax.ShapeDtypeStruct((frames, depth), jnp.bfloat16)] * parts,
        scratch_shapes=[
            pltpu.VMEM((2, step, width), jnp.bfloat16),
            pltpu.VMEM((row_blocks, span, width), jnp.bfloat16),
            pltpu.SemaphoreType.DMA((col_blocks,)),
        ],
        compiler_params=params_of(),
        cost_estimate=BRIEF,
        name="dproject",
    )(order, moments, gains, *sums, dpre, z, weight)
    return dz, level, merged, da


def weight_kernel(pieces, *refs):
    level_refs, dz_refs = refs[:pieces], refs[pieces : 2 * pieces]
    center_ref, source_ref, out_ref = refs[2 * pieces :]
    level = sum(level_ref[...] for level_ref in level_refs)
    center = jnp.transpose(jnp.broadcast_to(center_ref[2:3, :], (8, center_ref.shape[1])))[:, :1]
    terms = -center * level
    lo = 0
    for dz_ref in dz_refs:
        count = dz_ref.shape[0]
        terms += lax.dot_general(
            source_ref[lo : lo + count, :],
            dz_ref[...],
            (((0,), (0,)), ((), ())),
            preferred_element_type=jnp.float32,
        )
        lo += count
    out_ref[...] = terms.astype(jnp.bfloat16)


def weight_terms(source, moments, dz, levels):
    frames, rows = source.shape
    cols = dz[0].shape[1]
    tile = 512
    return pl.pallas_call(
        functools.partial(weight_kernel, len(dz)),
        grid=(rows // tile,),
        in_specs=[whole((1, cols))] * len(dz)
        + [whole(d.shape) for d in dz]
        + [
            pl.BlockSpec((3, tile), lambda i: (0, i)),
            pl.BlockSpec((frames, tile), lambda i: (0, i)),
        ],
        out_specs=pl.BlockSpec((tile, cols), lambda i: (i, 0)),
        out_shape=jax.ShapeDtypeStruct((rows, cols), jnp.bfloat16),
        compiler_params=params_of(),
        cost_estimate=BRIEF,
        name="weight",
    )(*levels, *dz, moments, source)


def small_kernel(total_frames, place, *refs):
    ins, outs = refs[:4], refs[4:]
    each = outs[0].shape[1]
    first = place[0] * each
    aligned = pl.multiple_of(first // LANES * LANES, LANES)
    turn = lax.rem(LANES - (first - aligned), LANES)

    def own(ref, row):
        return pltpu.roll(ref[row : row + 1, pl.ds(aligned, LANES)], turn, 1)[:, :each]

    for i in range(2):
        sums, moments = ins[2 * i : 2 * i + 2]
        rstd = lax.rsqrt(own(moments, 1) / total_frames + EPSILON)
        outs[3 * i][...] = own(sums, 1) * rstd
        outs[3 * i + 1][...] = own(sums, 0)
        outs[3 * i + 2][...] = own(sums, 2)


def small_gradients(place, each, total_frames, *values):
    results = pl.pallas_call(
        functools.partial(small_kernel, total_frames),
        in_specs=[SMEM] + [pl.BlockSpec(memory_space=pltpu.VMEM)] * 4,
        out_specs=[pl.BlockSpec(memory_space=pltpu.VMEM)] * 6,
        out_shape=[jax.ShapeDtypeStruct((1, each), jnp.float32)] * 6,
        cost_estimate=BRIEF,
        name="small",
    )(place, *values)
    results = [r.reshape(each) for r in results]
    return results[:3], results[3:]


def per_device(sizes, inputs, flags, w_one, *rest):
    gamma_one, beta_one, decay_one, w_two, gamma_two, beta_two, decay_two, cotangent = rest
    wide, narrow = sizes["wide"], sizes["narrow"]
    n = lax.axis_index("narrow")
    w = lax.axis_index("wide")
    frames = inputs.shape[0] // narrow
    part = inputs.shape[1]
    tiles = part // LANES
    total_frames = inputs.shape[0] * wide
    rows = frames // ROW_LEN
    first = w * inputs.shape[0] + n * frames
    keep = lax.dynamic_slice_in_dim(flags, first, frames, 0).reshape(rows, ROW_LEN)
    keep = (1 - keep).astype(jnp.float32)
    tie = lax.optimization_barrier

    def along(value, merge):
        return merge_all(value, merge, "narrow", narrow)

    def across(value, merge, open_end=False):
        return merge_all(value, merge, "wide", wide, open_end)

    own = jnp.stack([gamma_one, beta_one, decay_one, gamma_two, beta_two, decay_two])
    each = own.shape[1]
    spread = jnp.zeros((6, each * wide * narrow), jnp.float32)
    spread = lax.dynamic_update_slice_in_dim(spread, own, (n * wide + w) * each, 1)

    units = [(j, r) for j in range(tiles) for r in range(rows)]
    quarter = len(units) // 4
    groups_in = [
        ("line", units[:quarter]),
        ("line", units[quarter : 3 * quarter]),
        ("line", units[3 * quarter :]),
    ]
    eighth = len(units) // 8
    groups_out = [
        ("line", units[:eighth]),
        ("line", units[eighth : 5 * eighth]),
        ("line", units[5 * eighth : 6 * eighth]),
        ("line", units[6 * eighth :]),
    ]

    sliced = cotangent.reshape(narrow, rows, ROW_LEN, tiles, LANES)
    held = [jnp.stack([sliced[:, r, :, j] for j, r in group], 1) for _, group in groups_in]

    apart = [list(range(1, narrow)), [*range(2, narrow), 1]]
    in_step = [apart[0], apart[0]]

    def line_of(turns):
        return [n] + [n ^ jnp.where(w % 2 == 0, q, p) for p, q in zip(*turns, strict=True)]

    def along_line(blocks, turns=apart):
        came = blocks[:1]
        for k in range(1, narrow):
            pairs = [
                (i * narrow + j, i * narrow + (j ^ turns[1 - i % 2][k - 1]))
                for i in range(wide)
                for j in range(narrow)
            ]
            came.append(lax.ppermute(blocks[k], ("wide", "narrow"), pairs))
        return came

    line = line_of(apart)
    order = jnp.stack([jnp.asarray(q, jnp.int32) for q in line])
    last_line = line_of(in_step)
    last_order = jnp.stack([jnp.asarray(q, jnp.int32) for q in last_line])
    alone = jnp.zeros((1,), jnp.int32)

    split = frames // 4
    def frames_for(lo, hi):
        return [lax.dynamic_slice_in_dim(inputs, q * frames + lo, hi - lo, 0) for q in line]

    early = along_line(frames_for(0, split))
    late = frames_for(split, frames)
    shares = gather_rows([w_one, w_two], wide)
    held = [[lax.dynamic_index_in_dim(h, q, 0, keepdims=False) for q in line] for h in held]
    first = held[0]
    shares, early, late, held, spread, keep, first, order = tie(
        (shares, early, late, held, spread, keep, first, order)
    )
    late = along_line(late)
    gains = across(spread, add)
    for k in (1, 2):
        gains = gains + lax.ppermute(gains, "narrow", [(i, i ^ k) for i in range(narrow)])
    share_one, share_two = shares[0], shares[1]
    full_one = lax.all_gather(share_one, "wide", axis=0)
    full_one, first = tie((full_one, first))
    first = along_line(first)
    late, held, share_two, gains = tie((late, held, share_two, gains))
    gains_one, gains_two = gains[:3], gains[3:]
    full_two = lax.all_gather(share_two, "wide", axis=0)
    z_one, moments, source = project([early, late], order, full_one)
    moments, first = tie((moments, first))
    grads = [first]
    merge = merge_moments(frames)
    moments = along(moments, merge)
    moments, held = tie((moments, held))
    group = along_line(held[1])
    halves = across(moments, merge, True)
    plain = [("rows", None)]
    states_one, moments_one, ((h_one,),) = forward(
        z_one, halves, gains_one, keep, alone, plain, total_frames
    )
    h_one = h_one.reshape(frames, -1)
    z_two, moments = project([[h_one]], alone, full_two)
    moments, group = tie((moments, group))
    grads.append(group)
    merge = merge_moments(frames)
    moments = along(moments, merge)
    moments, held = tie((moments, held))
    group = along_line(held[2])
    halves = across(moments, merge, True)
    states_two, moments_two, h_two = forward(
        z_two, halves, gains_two, keep, order, groups_out, total_frames
    )
    grads.append(group)

    second = [along_line(h_two[0])]
    dpre, sums = backward(
        grads, order, groups_in, states_two, z_two, moments_two, gains_two, keep, gains_two
    )
    sums, second[0] = tie((sums, second[0]))
    sums = along(sums, add)
    sums, h_two = tie((sums, h_two))
    group = along_line(h_two[1])
    halves = across(sums, add, True)
    dz_two, level_two, sums_two, (dh_one,) = dproject(
        dpre, z_two, moments_two, gains_two, halves, full_two, alone, total_frames, 0, frames
    )
    terms_two = weight_terms(h_one, moments_two, [dz_two], [level_two])
    terms_two, third = tie((terms_two, h_two[2]))
    third = along_line(third)
    terms_two, dh_one, group = tie((terms_two, dh_one, group))
    second.append(group)
    plane_two = lax.psum_scatter(terms_two, "wide", scatter_dimension=0, tiled=True)
    dh_one = dh_one.reshape(rows, ROW_LEN, -1)
    dpre, sums = backward(
        [[dh_one]], alone, plain, states_one, z_one, moments_one, gains_one, keep, level_two
    )
    sums, third = tie((sums, third))
    second.append(third)
    sums = along(sums, add)
    sums, h_two = tie((sums, h_two))
    group = along_line(h_two[3])
    halves = across(sums, add, True)
    back = functools.partial(
        dproject, dpre, z_one, moments_one, gains_one, halves, full_one, last_order, total_frames
    )
    split = frames // 4
    dz_early, level_early, sums_one, da_early = back(0, split)
    da_early, group = tie((da_early, group))
    second.append(group)
    da_early = along_line(da_early, in_step)
    dz_late, level_late, _, da_late = back(split, frames)
    terms_one = weight_terms(source, moments_one, [dz_early, dz_late], [level_early, level_late])
    levels = (level_early, level_late)
    da_early, da_late, terms_one, plane_two, levels, second = tie(
        (da_early, da_late, terms_one, plane_two, levels, second)
    )
    plane_one = lax.psum_scatter(terms_one, "wide", scatter_dimension=0, tiled=True)
    da_late = along_line(da_late, in_step)
    da_late[1], second, moments_one, moments_two, sums_one, sums_two, plane_two = tie(
        (da_late[1], second, moments_one, moments_two, sums_one, sums_two, plane_two)
    )
    parts = {}
    for (kind, group), came in zip(groups_out, second, strict=True):
        if kind == "line":
            stacked = jnp.stack(came)
            places = []
            for q in range(narrow):
                turn = n ^ q
                shifted = jnp.where(turn == 1, narrow - 1, jnp.maximum(turn - 1, 0))
                places.append(jnp.where(w % 2 == 0, shifted, turn))
            came = [
                jnp.stack(
                    [lax.dynamic_index_in_dim(stacked, p, 0, keepdims=False) for p in places]
                )
            ]
        for u, unit in enumerate(group):
            parts[unit] = came[0][:, u]
    whole_two = jnp.stack(
        [jnp.concatenate([parts[j, r] for j in range(tiles)], -1) for r in range(rows)], 1
    )
    whole_two = whole_two.reshape(inputs.shape).astype(jnp.float32)
    output = (inputs.astype(jnp.float32) + whole_two).astype(jnp.bfloat16)

    output, levels = tie((output, levels))

    span = plane_one.shape[0]

    blocks = plane_two.reshape(span, narrow, part).transpose(1, 0, 2)
    came_two = lax.all_to_all(blocks, "narrow", split_axis=0, concat_axis=0)
    came_two = [came_two[i] for i in range(narrow)]
    level_one = levels[0] + levels[1]
    k = wide // 2
    while k:
        level_one = level_one + lax.ppermute(level_one, "wide", [(i, i ^ k) for i in range(wide)])
        k //= 2
    columns = [lax.dynamic_slice_in_dim(plane_one, q * part, part, 1) for q in last_line]
    columns, level_one = tie((columns, level_one))
    came_one = along_line(columns, in_step)
    k = narrow // 2
    while k:
        level_one = level_one + lax.ppermute(
            level_one, "narrow", [(i, i ^ k) for i in range(narrow)]
        )
        k //= 2

    grad_inputs = jnp.zeros(inputs.shape, jnp.float32)
    for lo, came in ((0, da_early), (split, da_late)):
        for q, block in zip(last_line, came, strict=True):
            at = q * frames + lo
            own = lax.dynamic_slice_in_dim(cotangent, at, block.shape[0], 0).astype(jnp.float32)
            grad_inputs = lax.dynamic_update_slice_in_dim(
                grad_inputs, own + block.astype(jnp.float32), at, 0
            )
    came_two, came_one = tie((came_two, came_one))
    dw_two = sum(block.astype(jnp.float32) for block in came_two)
    dw_one = sum(block.astype(jnp.float32) for block in came_one)

    def restored(weight, moments, level, row):
        rows_of = lax.dynamic_slice(moments, (2, w * span), (1, span)).reshape(span, 1)
        return weight + rows_of * lax.dynamic_slice(level, (row, n * part), (1, part))

    dw_one = restored(dw_one, moments_one, level_one, 0)
    dw_two = restored(dw_two, moments_two, sums_one, 3)

    place = jnp.asarray(n * wide + w, jnp.int32).reshape(1)
    small_one, small_two = small_gradients(
        place, each, total_frames, sums_one, moments_one, sums_two, moments_two
    )
    return output, grad_inputs, dw_one, *small_one, dw_two, *small_two


def solution(mesh):
    neurons = P(("narrow", "wide"))
    frames = P("wide", "narrow")
    weight = P(None, "narrow")
    small = (neurons, neurons, neurons)
    return jax.shard_map(
        functools.partial(per_device, dict(mesh.shape)),
        mesh=mesh,
        in_specs=(frames, P(), weight, *small, weight, *small, frames),
        out_specs=(frames, frames, frames, *small, frames, *small),
        check_vma=False,
    )
```
